128 devices in a mesh: row: 8 (over x, z_hi), col: 16 (over z_lo, y, core).
Axes of the slice: x: 4, y: 4, z: 4 (z_hi: 2, z_lo: 2; z = z_hi * 2 + z_lo), core: 2. Of those that a mesh axis runs over, the one named last changes fastest.
Arguments:
- activations: bfloat16 [2048, 16384], P(('row', 'col')), may hold values from -6 to 6
- labels: int32 [2048], P(('row', 'col')), may hold values from 0 to 63
- valid: int32 [2048], P(('row', 'col')), may hold values 0 or 1
- class_weight: float32 [64], replicated, may hold values from 0.25 to 4
Outputs:
- gram: float32 [16384, 16384], P('row', 'col')
- class_means: float32 [64, 16384], P(None, ('row', 'col'))
The draws below stay inside these ranges and needn't reach their ends.
All inputs are finite; a program needn't handle non-finite values. No bound on the sum of `valid` on one device may be relied on, other than what follows from the above.
Results may differ from the reference program's by a relative error of at most 0.0028.
Values may be sent and summed in bfloat16 or wider, within the bound.
A program may use at most 128 MiB of HBM per device.

```python
import math
import jax
import jax.numpy as jnp
from jax import lax

D = 16384
CLASSES = 64
TOKENS = 2048


def set_ends(result, stream_key, low, top_value):
    longest = result.shape.index(max(result.shape))
    spots = []
    for shift in (0, 1):
        where = [jax.random.randint(jax.random.fold_in(stream_key, axis), (), 0, length) for axis, length in enumerate(result.shape)]
        where[longest] = (where[longest] + shift) % result.shape[longest]
        spots.append(tuple(where))
    return result.at[spots[0]].set(low).at[spots[1]].set(top_value)


def steps_of(rng, shape, split, least, top_value):
    factor_of, own = 1.0, jax.random.fold_in(rng, 6)
    for dim, blocks in split:
        steps = jnp.exp(jax.random.uniform(jax.random.fold_in(own, dim), (blocks,), jnp.float32, least / len(split), top_value / len(split)))
        factor_of = factor_of * jnp.repeat(steps, shape[dim] // blocks).reshape([-1 if axis == dim else 1 for axis in range(len(shape))])
    return factor_of


def gaussian(key, extent, spread, reach, pieces=(), kind=jnp.bfloat16):
    drawn = jax.random.normal(key, extent, jnp.float32) * spread
    if len(pieces) > 0:
        drawn = steps_of(key, extent, pieces, -0.22, 0.18) * drawn
    return jnp.clip(drawn, min=-reach, max=reach).astype(kind)


def setup_inputs(seed: int = 0) -> dict:
    arg_keys = jax.random.split(jax.random.key(seed), 5)
    activations = gaussian(arg_keys[0], (TOKENS, D), 1.0, 6.0, ((0, 128),))
    labels = set_ends(jax.random.randint(arg_keys[1], (TOKENS,), 0, CLASSES), jax.random.fold_in(arg_keys[1], 1), 0, CLASSES - 1).astype(jnp.int32)
    valid = set_ends((jax.random.randint(arg_keys[2], (TOKENS,), 0, 4) < 3).astype(jnp.int32), jax.random.fold_in(arg_keys[2], 1), 0, 1)
    class_weight = jnp.clip(jnp.exp(jax.random.uniform(arg_keys[3], (CLASSES,), jnp.float32, math.log(0.25), math.log(4.0))), 0.25, 4.0)
    return dict(activations=activations, labels=labels, valid=valid, class_weight=class_weight)


def reference(activations, labels, valid, class_weight):
    onehot = (labels[:, None] == jnp.arange(CLASSES, dtype=jnp.int32)[None, :]).astype(jnp.float32)
    kept = onehot * valid.astype(jnp.float32)[:, None]
    weights = jnp.dot(kept, class_weight, precision=lax.Precision.HIGHEST)
    counts = jnp.sum(kept, axis=0)
    dense = activations.astype(jnp.float32)
    scaled = (weights[:, None] * dense).astype(jnp.bfloat16).astype(jnp.float32)
    block_width = D // 8

    def one_block(index):
        rows = lax.dynamic_slice_in_dim(dense, index * block_width, block_width, 1)
        return jnp.dot(rows.T, scaled, precision=lax.Precision.HIGHEST)

    gram = lax.map(one_block, jnp.arange(8, dtype=jnp.int32)).reshape(D, D) / float(TOKENS)
    sums = jnp.dot(kept.T, dense, precision=lax.Precision.HIGHEST)
    class_means = sums / (counts[:, None] + 1.0)
    return gram, class_means
```

```python
import jax
import jax.numpy as jnp
from jax import lax
from jax.experimental import pallas as pl
from jax.experimental.pallas import tpu as pltpu
from jax.sharding import PartitionSpec as P

MESH = pl.DeviceIdType.MESH

OFF = (0, 1, 3, 2)
NEG = (0, 2, 1, 3)
UPWARD = (0, 3)


def pair(px, py, core, zl):
    return ((px * 4 + py) * 2 + core) * 2 + zl


def kernel(x_ref, lab_ref, val_ref, cw_ref, gram_ref, means_ref, xs, rp, cp, sc, sums, send, recv, local):
    tok, width = x_ref.shape
    block = width // 8
    half = block // 2
    row, col = lax.axis_index("row"), lax.axis_index("col")
    x, zh = row // 2, row % 2
    zl, y, core = col // 8, (col // 2) % 4, col % 2

    def flip(v, by):
        return (1 - v) if by else v

    def device(ox=0, oy=0, ozh=0, ozl=0, ok=0):
        r = ((x + ox) % 4) * 2 + flip(zh, ozh)
        c = (flip(zl, ozl) * 4 + (y + oy) % 4) * 2 + flip(core, ok)
        return r, c

    stage = [
        pltpu.make_async_copy(
            x_ref.at[:, pl.ds(b * block, block)], xs.at[b, :, pl.ds(0, block)], local.at[b]
        )
        for b in range(8)
    ]
    for s in stage:
        s.start()

    row_peers = [(p, ozh) for p in range(4) for ozh in range(2) if (p, ozh) != (0, 0)]
    col_peers = [
        (p, ozl, ok)
        for p in range(4)
        for ozl in range(2)
        for ok in range(2)
        if (p, ozl, ok) != (0, 0, 0)
    ]
    barrier = pltpu.get_barrier_semaphore()
    for p, ozh in row_peers:
        pl.semaphore_signal(barrier, inc=1, device_id=device(ox=OFF[p], ozh=ozh), device_id_type=MESH)
    for p, ozl, ok in col_peers:
        pl.semaphore_signal(
            barrier, inc=1, device_id=device(oy=OFF[p], ozl=ozl, ok=ok), device_id_type=MESH
        )

    diag = lax.broadcasted_iota(jnp.int32, (tok, tok), 0) == lax.broadcasted_iota(
        jnp.int32, (tok, tok), 1
    )
    lab = jnp.sum(jnp.where(diag, lab_ref[...].astype(jnp.float32), 0.0), axis=1, keepdims=True)
    val = jnp.sum(jnp.where(diag, val_ref[...].astype(jnp.float32), 0.0), axis=1, keepdims=True)
    lanes = lax.broadcasted_iota(jnp.int32, (tok, 128), 1).astype(jnp.float32)
    kept = jnp.where(lanes == lab, val, 0.0).astype(jnp.bfloat16)
    for b in range(8):
        xs[b, :, block:] = kept
    for s in stage:
        s.wait()
    pl.semaphore_wait(barrier, len(row_peers) + len(col_peers))

    copies = {}

    def go(name, src, dst, to):
        i = len(copies)
        copies[name] = pltpu.make_async_remote_copy(
            src_ref=src,
            dst_ref=dst,
            send_sem=send.at[i],
            recv_sem=recv.at[i],
            device_id=to,
            device_id_type=MESH,
        )
        copies[name].start()

    own_r = pltpu.make_async_copy(xs.at[row], rp.at[0, 0], local.at[0])
    own_r.start()
    own_c = pltpu.make_async_copy(
        xs.at[col // 2, :, pl.ds(pl.multiple_of(core * half, half), half)], cp.at[0, 0], local.at[1]
    )
    own_c.start()

    def first_r(p, ozh):
        r, c = device(ox=OFF[p], ozh=ozh)
        go(("r", p, ozh), xs.at[r], rp.at[pair(NEG[p], 0, 0, 0), ozh], (r, c))

    def first_c(p, ozl, ok):
        r, c = device(oy=OFF[p], ozl=ozl, ok=ok)
        go(
            ("c", p, ozl, ok),
            xs.at[c // 2, :, pl.ds(pl.multiple_of((c % 2) * half, half), half)],
            cp.at[pair(0, NEG[p], ok, ozl), 0],
            (r, c),
        )

    for p in range(4):
        for ozh in range(2):
            if (p, ozh) in row_peers:
                first_r(p, ozh)
        for ozl in range(2):
            for ok in range(2):
                if (p, ozl, ok) in col_peers:
                    first_c(p, ozl, ok)
    own_r.wait()
    own_c.wait()

    def r_of(px, py, q):
        return rp.at[pair(px, py, 0, q)]

    def c_of(px, py, q):
        return cp.at[pl.ds(pair(px, py, 0, 0), 4), q]

    def ring_r(px, q):
        go(("ru", px, q), r_of(px, 0, q), r_of(px, 2, q), device(oy=1))
        go(("rd", px, q), r_of(px, 0, q), r_of(px, 1, q), device(oy=3))

    def ring_c(py, q):
        go(("cu", py, q), c_of(0, py, q), c_of(2, py, q), device(ox=1))
        go(("cd", py, q), c_of(0, py, q), c_of(1, py, q), device(ox=3))

    def twin(px, py):
        two = pl.ds(pair(px, py, 0, 0), 2)
        go(("t", px, py), rp.at[two], rp.at[pl.ds(pair(px, py, 1, 0), 2)], device(ok=1))

    for p in range(4):
        for ozh in range(2):
            if (p, ozh) in row_peers:
                copies["r", NEG[p], ozh].wait_recv()
        go(("rz", p), r_of(p, 0, 0), r_of(p, 0, 1), device(ozl=1))
        ring_r(p, 0)
        for ozl in range(2):
            for ok in range(2):
                if (p, ozl, ok) in col_peers:
                    copies["c", NEG[p], ozl, ok].wait_recv()
        go(("cz", p), c_of(0, p, 0), c_of(0, p, 1), device(ozh=1))
        ring_c(p, 0)
    for p in range(4):
        copies["rz", p].wait_recv()
        ring_r(p, 1)
        twin(p, 0)
        copies["cz", p].wait_recv()
        ring_c(p, 1)

    for q in range(2):
        for p in range(4):
            copies["ru", p, q].wait_recv()
            if p in UPWARD:
                go(("rf", p, q), r_of(p, 2, q), r_of(p, 3, q), device(oy=1))
            copies["cu", p, q].wait_recv()
            if p in UPWARD:
                go(("cf", p, q), c_of(2, p, q), c_of(3, p, q), device(ox=1))
            copies["rd", p, q].wait_recv()
            if p not in UPWARD:
                go(("rf", p, q), r_of(p, 1, q), r_of(p, 3, q), device(oy=3))
            copies["cd", p, q].wait_recv()
            if p not in UPWARD:
                go(("cf", p, q), c_of(1, p, q), c_of(3, p, q), device(ox=3))
            if q == 1:
                twin(p, 1)
                twin(p, 2)

    tile = 256
    lane = pl.multiple_of(col * 128, 128)

    def multiply(px, py, n):
        start, n = pair(px, py, 0, 0), n * 4
        rows = n * 2 * tok
        first = (px, py) == (0, 0)
        pairs = pl.ds(start, n)
        k = rp[pairs, :, :, block:].reshape(rows, 128)
        w = jnp.sum(k[:, :64].astype(jnp.float32) * cw_ref[...], axis=1, keepdims=True)
        sc[:rows, :] = (w * cp[pairs].reshape(rows, half).astype(jnp.float32)).astype(jnp.bfloat16)
        mine = rp[pairs, :, :, pl.ds(lane, 128)].reshape(rows, 128)
        both = jnp.concatenate([mine, jnp.ones((rows, 128), jnp.bfloat16)], axis=1)
        part = over_rows(k, both)
        if first:
            sums[...] = part
        else:
            sums[...] += part

        @pl.loop(0, block // tile)
        def _(i):
            at = pl.ds(pl.multiple_of(i * tile, tile), tile)
            part = over_rows(rp[pairs, :, :, at].reshape(rows, tile), sc[:rows, :])
            if first:
                gram_ref[at, :] = part
            else:
                gram_ref[at, :] += part

    for px in range(3):
        for py in range(3):
            copies["t", px, py].wait_recv()
        multiply(px, 0, 3)
    for p in range(4):
        for q in range(2):
            copies["rf", p, q].wait_recv()
        twin(p, 3)
    for py in range(3):
        copies["t", 3, py].wait_recv()
        for q in range(2):
            copies["cf", py, q].wait_recv()
    multiply(3, 0, 3)
    for px in range(3):
        copies["t", px, 3].wait_recv()
        multiply(px, 3, 1)
    copies["t", 3, 3].wait_recv()
    for q in range(2):
        copies["cf", 3, q].wait_recv()
    multiply(3, 3, 1)
    means_ref[...] = sums[:64, :128] / (sums[:64, 128:] + 1.0)
    for c in copies.values():
        c.wait_send()


def over_rows(left, right):
    return lax.dot_general(
        left, right, (((0,), (0,)), ((), ())), preferred_element_type=jnp.float32
    )


def body(activations, labels, valid, class_weight):
    tok, width = activations.shape
    total = tok * lax.axis_size("row") * lax.axis_size("col")
    classes = class_weight.shape[0]
    block = width // 8
    vmem = pl.BlockSpec(memory_space=pltpu.VMEM)
    gram, means = pl.pallas_call(
        kernel,
        out_shape=(
            pltpu.VMEM((block, block // 2), jnp.float32),
            jax.ShapeDtypeStruct((classes, 128), jnp.float32),
        ),
        in_specs=[pl.BlockSpec(memory_space=pl.ANY), vmem, vmem, vmem],
        out_specs=(vmem, vmem),
        scratch_shapes=[
            pltpu.VMEM((8, tok, block + 128), jnp.bfloat16),
            pltpu.VMEM((64, 2, tok, block + 128), jnp.bfloat16),
            pltpu.VMEM((64, 2, tok, block // 2), jnp.bfloat16),
            pltpu.VMEM((512, block // 2), jnp.bfloat16),
            pltpu.VMEM((128, 256), jnp.float32),
            pltpu.SemaphoreType.DMA((96,)),
            pltpu.SemaphoreType.DMA((96,)),
            pltpu.SemaphoreType.DMA((8,)),
        ],
        compiler_params=pltpu.CompilerParams(
            collective_id=0, has_side_effects=True, vmem_limit_bytes=40 * 1024 * 1024
        ),
    )(
        activations,
        labels.reshape(1, tok),
        valid.reshape(1, tok),
        class_weight.reshape(1, classes),
    )
    return gram / float(total), means


def solution(mesh):
    in_specs = (P(("row", "col"), None), P(("row", "col")), P(("row", "col")), P())
    out_specs = (P("row", "col"), P(None, ("row", "col")))
    return jax.shard_map(body, mesh=mesh, in_specs=in_specs, out_specs=out_specs, check_vma=False)
```

```python
import jax
import jax.numpy as jnp
from jax import lax
from jax.experimental import pallas as pl
from jax.experimental.pallas import tpu as pltpu
from jax.sharding import PartitionSpec as P

MESH = pl.DeviceIdType.MESH

OFF = (0, 1, 3, 2)
NEG = (0, 2, 1, 3)
UPWARD = (0, 3)
EARLY = (((0, 0), (0, 1)), ((0, 2), (1, 0)))
MIDDLE = (((2, 0), (1, 1)), ((1, 2), (2, 1)))
LATE = (((2, 2), (0, 3)), ((3, 0), (1, 3)))
LAST = ((3, 1), (2, 3), (3, 2), (3, 3))


def over_rows(left, right):
    return lax.dot_general(
        left, right, (((0,), (0,)), ((), ())), preferred_element_type=jnp.float32
    )


def at_group(px, py):
    return px * 4 + py


def rows_of(ref, groups, lanes):
    parts = [ref[at_group(*g), :, :, :, lanes] for g in groups]
    parts = [p.reshape(-1, p.shape[-1]) for p in parts]
    return parts[0] if len(parts) == 1 else jnp.concatenate(parts, axis=0)


def class_sums(rp, groups, block, lane):
    kept = rows_of(rp, groups, pl.ds(block, 128))
    mine = rows_of(rp, groups, pl.ds(lane, 128))
    both = jnp.concatenate([mine, jnp.ones(mine.shape, jnp.bfloat16)], axis=1)
    return kept, over_rows(kept, both)


def exchange(
    x_hbm, lab_hbm, val_hbm, cw_hbm, acc, sums, rp, last, xs, cp, tb, sc, lab_ref, val_ref, cw_ref, send, recv, local
):
    tok, width = x_hbm.shape
    block = width // 8
    half = block // 2
    row, col = lax.axis_index("row"), lax.axis_index("col")
    x, zh = row // 2, row % 2
    zl, y, core = col // 8, (col // 2) % 4, col % 2

    def flip(v, by):
        return (1 - v) if by else v

    def device(ox=0, oy=0, ozh=0, ozl=0, ok=0):
        r = ((x + ox) % 4) * 2 + flip(zh, ozh)
        c = (flip(zl, ozl) * 4 + (y + oy) % 4) * 2 + flip(core, ok)
        return r, c

    stage = [
        pltpu.make_async_copy(
            x_hbm.at[:, pl.ds(b * block, block)], xs.at[b, :, pl.ds(0, block)], local.at[b]
        )
        for b in range(8)
    ]
    small = [
        pltpu.make_async_copy(s, d, local.at[8 + i])
        for i, (s, d) in enumerate(((lab_hbm, lab_ref), (val_hbm, val_ref), (cw_hbm, cw_ref)))
    ]
    for s in small + stage:
        s.start()

    row_peers = [(p, h) for p in range(4) for h in range(2) if (p, h) != (0, 0)]
    col_peers = [(p, ok) for p in range(4) for ok in range(2) if (p, ok) != (0, 0)]
    peers = (
        [device(ox=OFF[p], ozh=h, ozl=h) for p, h in row_peers]
        + [device(oy=OFF[p], ok=ok) for p, ok in col_peers]
        + [device(ozl=1), device(ozh=1)]
    )
    barrier = pltpu.get_barrier_semaphore()
    for peer in peers:
        pl.semaphore_signal(barrier, inc=1, device_id=peer, device_id_type=MESH)

    for s in small:
        s.wait()
    diag = lax.broadcasted_iota(jnp.int32, (tok, tok), 0) == lax.broadcasted_iota(
        jnp.int32, (tok, tok), 1
    )
    lab = jnp.sum(jnp.where(diag, lab_ref[...].astype(jnp.float32), 0.0), axis=1, keepdims=True)
    val = jnp.sum(jnp.where(diag, val_ref[...].astype(jnp.float32), 0.0), axis=1, keepdims=True)
    lanes = lax.broadcasted_iota(jnp.int32, (tok, 128), 1).astype(jnp.float32)
    kept = jnp.where(lanes == lab, val, 0.0).astype(jnp.bfloat16)
    for b in range(8):
        xs[b, :, block:] = kept
    for s in stage:
        s.wait()
    own = [
        pltpu.make_async_copy(xs.at[row], rp.at[0, 0, 0], local.at[0]),
        pltpu.make_async_copy(
            xs.at[zl * 4 + y, :, pl.ds(pl.multiple_of(core * half, half), half)],
            cp.at[0, 0, 0],
            local.at[1],
        ),
        pltpu.make_async_copy(
            xs.at[(1 - zl) * 4 + y, :, pl.ds(pl.multiple_of(core * half, half), half)],
            tb.at[0, 0],
            local.at[2],
        ),
    ]
    for s in own:
        s.start()
    pl.semaphore_wait(barrier, len(peers))

    copies = {}

    def go(name, src, dst, to):
        i = len(copies)
        copies[name] = pltpu.make_async_remote_copy(
            src_ref=src,
            dst_ref=dst,
            send_sem=send.at[i],
            recv_sem=recv.at[i],
            device_id=to,
            device_id_type=MESH,
        )
        copies[name].start()

    def got(*names):
        for n in names:
            copies[n].wait_recv()

    for p in range(4):
        for h in (1, 0):
            if (p, h) in row_peers:
                to = device(ox=OFF[p], ozh=h, ozl=h)
                go(("r", p, h), xs.at[to[0]], rp.at[at_group(NEG[p], 0), 0, h], to)
        for ok in range(2):
            if (p, ok) in col_peers:
                r, c = device(oy=OFF[p], ok=ok)
                lane = pl.ds(pl.multiple_of((c % 2) * half, half), half)
                y_to = (y + OFF[p]) % 4
                go(("cs", p, ok), xs.at[zl * 4 + y_to, :, lane], cp.at[at_group(0, NEG[p]), ok, 0], (r, c))
                go(("cf", p, ok), xs.at[(1 - zl) * 4 + y_to, :, lane], tb.at[NEG[p], ok], (r, c))
    for s in own:
        s.wait()

    def r_of(px, py, q):
        return rp.at[at_group(px, py), 0, pl.ds(2 * q, 2)]

    def c_of(px, py, q):
        return cp.at[at_group(px, py), :, pl.ds(2 * q, 2)]

    def ring_r(px, q):
        go(("ru", px, q), r_of(px, 0, q), r_of(px, 2, q), device(oy=1))
        go(("rd", px, q), r_of(px, 0, q), r_of(px, 1, q), device(oy=3))

    def ring_c(py, q):
        go(("cu", py, q), c_of(0, py, q), c_of(2, py, q), device(ox=1))
        go(("cd", py, q), c_of(0, py, q), c_of(1, py, q), device(ox=3))

    def twin(px, py):
        g = at_group(px, py)
        go(("t", px, py), rp.at[g, 0], rp.at[g, 1], device(ok=1))

    for p in range(4):
        got(*[("r", NEG[p], h) for h in range(2) if (p, h) in row_peers])
        go(("rz", p), r_of(p, 0, 0), r_of(p, 0, 1), device(ozl=1))
        ring_r(p, 0)
        got(*[(n, NEG[p], ok) for n in ("cs", "cf") for ok in range(2) if (p, ok) in col_peers])
        g = at_group(0, p)
        go(("z1", p), tb.at[p], cp.at[g, :, 1], device(ozh=1, ozl=1))
        go(("z2", p), tb.at[p], cp.at[g, :, 2], device(ozl=1))
        go(("z3", p), cp.at[g, :, 0], cp.at[g, :, 3], device(ozh=1))
    for p in range(4):
        got(("z1", p))
        ring_c(p, 0)
        got(("rz", p))
        ring_r(p, 1)
        twin(p, 0)
    for p in range(4):
        got(("z2", p), ("z3", p))
        ring_c(p, 1)

    lane = pl.multiple_of(col * 128, 128)

    def weigh(groups, into, at):
        kept, part = class_sums(rp, groups, block, lane)
        w = jnp.sum(kept[:, :64].astype(jnp.float32) * cw_ref[...], axis=1, keepdims=True)
        right = rows_of(cp, groups, slice(None)).astype(jnp.float32)
        into[at, :] = (w * right).astype(jnp.bfloat16)
        return part

    def multiply(groups, first=False):
        rows = len(groups) * 8 * tok
        part = weigh(groups, sc, pl.ds(0, rows))
        if first:
            sums[...] = part
        else:
            sums[...] += part

        @pl.loop(0, 2)
        def _(i):
            at = pl.ds(pl.multiple_of(i * half, half), half)
            left = rows_of(rp, groups, at)
            for j in range(half // 256):
                to = pl.ds(j * 256, 256)
                part = over_rows(left, sc[:rows, to])
                if first:
                    acc[at, to] = part
                else:
                    acc[at, to] += part

    def ring_step(q, p):
        got(("ru", p, q), ("rd", p, q))
        if p in UPWARD:
            go(("rf", p, q), r_of(p, 2, q), r_of(p, 3, q), device(oy=1))
        else:
            go(("rf", p, q), r_of(p, 1, q), r_of(p, 3, q), device(oy=3))
        got(("cu", p, q), ("cd", p, q))
        if p in UPWARD:
            go(("cx", p, q), c_of(2, p, q), c_of(3, p, q), device(ox=1))
        else:
            go(("cx", p, q), c_of(1, p, q), c_of(3, p, q), device(ox=3))
        if q == 1:
            twin(p, 1)
            twin(p, 2)

    def ring_end(p):
        got(("rf", p, 0), ("rf", p, 1))
        twin(p, 3)
        got(("cx", p, 0), ("cx", p, 1))

    for p in range(4):
        ring_step(0, p)
    ring_step(1, 0)
    got(*[("t", px, 0) for px in range(4)], ("t", 0, 1), ("t", 0, 2))
    multiply(EARLY[0], True)
    ring_step(1, 1)
    multiply(EARLY[1])
    ring_step(1, 2)
    got(("t", 1, 1), ("t", 1, 2), ("t", 2, 1), ("t", 2, 2))
    multiply(MIDDLE[0])
    ring_step(1, 3)
    multiply(MIDDLE[1])
    ring_end(0)
    got(("t", 0, 3))
    multiply(LATE[0])
    ring_end(1)
    got(("t", 1, 3))
    multiply(LATE[1])
    ring_end(2)
    ring_end(3)
    got(("t", 2, 3), ("t", 3, 3), ("t", 3, 1), ("t", 3, 2))
    for i, g in enumerate(LAST):
        sums[...] += weigh([g], last, pl.ds(i * 8 * tok, 8 * tok))
    for c in copies.values():
        c.wait_send()


def finish(acc, sums, rp, last, gram_hbm, means, out, sems):
    rows, half = acc.shape
    total = 16 * 8 * rp.shape[3]
    writes = []
    for i in range(2):
        at = pl.ds(i * half, half)
        left = rows_of(rp, LAST, at)
        for j in range(half // 256):
            to = pl.ds(j * 256, 256)
            out[at, to] = (acc[at, to] + over_rows(left, last[:, to])) / float(total)
            n = len(writes)
            writes.append(pltpu.make_async_copy(out.at[at, to], gram_hbm.at[at, to], sems.at[n]))
            writes[n].start()
    means[...] = sums[:64, :128] / (sums[:64, 128:] + 1.0)
    for w in writes:
        w.wait()


def body(activations, labels, valid, class_weight):
    tok, width = activations.shape
    classes = class_weight.shape[0]
    block = width // 8
    half = block // 2
    vmem = pl.BlockSpec(memory_space=pltpu.VMEM)
    hbm = pl.BlockSpec(memory_space=pltpu.HBM)
    parts = pl.pallas_call(
        exchange,
        out_shape=(
            pltpu.VMEM((block, half), jnp.float32),
            pltpu.VMEM((128, 256), jnp.float32),
            pltpu.VMEM((16, 2, 4, tok, block + 128), jnp.bfloat16),
            pltpu.VMEM((len(LAST) * 8 * tok, half), jnp.bfloat16),
        ),
        in_specs=[hbm] * 4,
        out_specs=(vmem,) * 4,
        scratch_shapes=[
            pltpu.VMEM((8, tok, block + 128), jnp.bfloat16),
            pltpu.VMEM((16, 2, 4, tok, half), jnp.bfloat16),
            pltpu.VMEM((4, 2, tok, half), jnp.bfloat16),
            pltpu.VMEM((2 * 8 * tok, half), jnp.bfloat16),
            pltpu.VMEM((1, tok), jnp.int32),
            pltpu.VMEM((1, tok), jnp.int32),
            pltpu.VMEM((1, classes), jnp.float32),
            pltpu.SemaphoreType.DMA((101,)),
            pltpu.SemaphoreType.DMA((101,)),
            pltpu.SemaphoreType.DMA((11,)),
        ],
        compiler_params=pltpu.CompilerParams(
            collective_id=0, has_side_effects=True, vmem_limit_bytes=12 * 1024 * 1024
        ),
    )(
        *[
            pltpu.with_memory_space_constraint(a, pltpu.HBM)
            for a in (
                activations,
                labels.reshape(1, tok),
                valid.reshape(1, tok),
                class_weight.reshape(1, classes),
            )
        ]
    )
    return pl.pallas_call(
        finish,
        out_shape=(
            jax.ShapeDtypeStruct((block, half), jnp.float32),
            jax.ShapeDtypeStruct((classes, 128), jnp.float32),
        ),
        in_specs=[vmem] * 4,
        out_specs=(hbm, vmem),
        scratch_shapes=[pltpu.VMEM((block, half), jnp.float32), pltpu.SemaphoreType.DMA((8,))],
        compiler_params=pltpu.CompilerParams(vmem_limit_bytes=14 * 1024 * 1024),
    )(*parts)


def solution(mesh):
    in_specs = (P(("row", "col"), None), P(("row", "col")), P(("row", "col")), P())
    out_specs = (P("row", "col"), P(None, ("row", "col")))
    return jax.shard_map(body, mesh=mesh, in_specs=in_specs, out_specs=out_specs, check_vma=False)
```

```python
import jax
import jax.numpy as jnp
from jax import lax
from jax.experimental import pallas as pl
from jax.experimental.pallas import tpu as pltpu
from jax.sharding import PartitionSpec as P

MESH = pl.DeviceIdType.MESH

OFF = (0, 1, 3, 2)
NEG = (0, 2, 1, 3)
UPWARD = (0, 3)
PARTS = ((0, 1), (1, 1), (2, 2))
HALVES = ((0, 2), (2, 2))
PARTS_OF = ((0, 1), (2,))
CHUNKS = (
    ((0, 0, 0, 4), (0, 1, 0, 4)),
    ((0, 2, 0, 4), (1, 0, 0, 4)),
    ((2, 0, 0, 4), (1, 1, 0, 4)),
    ((1, 2, 0, 4), (2, 1, 0, 4)),
    ((2, 2, 0, 4), (0, 3, 0, 4)),
    ((3, 0, 0, 4), (1, 3, 0, 4)),
    ((3, 1, 0, 4), (2, 3, 0, 2), (3, 2, 0, 2)),
)
LAST = ((3, 3, 0, 4), (2, 3, 2, 2), (3, 2, 2, 2))


ORDER = tuple(
    tuple(int(v) if v.isdigit() else v for v in step.split())
    for step in (
        "c 3 1 1", "c 0 1 1", "c 0 1 0", "c 2 1 1", "r 1 1", "c 1 0 1", "c 1 0 0", "c 3 0 0", "rz 0 0",
        "r 1 0", "r 0 1", "k1", "cu 0 0", "c 2 0 0", "z3 0", "c 2 0 1", "r 2 0", "z2 0", "ru 0 0",
        "c 1 1 0", "z1 0", "c 3 1 0", "r 3 0", "rd 0 0", "r 3 1", "c 2 1 0", "c 1 1 1", "r 2 1", "ru 0 1",
        "rd 1 0", "rz 0 1", "rd 1 1", "cd 1 0", "z1 2", "ru 2 0", "rz 1 0", "rz 1 1", "cu 0 2", "c 3 0 1",
        "k2", "rd 2 0", "cd 0 0", "ru 3 0", "cu 0 1", "cd 0 2", "z2 1", "rd 0 1", "cd 0 1", "ru 0 2",
        "z3 1", "z1 1", "cd 2 0", "cd 2 1", "cu 1 0", "rd 1 2", "rd 2 1", "rf 0 0", "z3 3", "z2 2",
        "rz 2 1", "t 1 0", "z3 2", "cx 0 1", "t 0 2", "k3", "z2 3", "z1 3", "rd 0 2", "rz 2 0", "rf 0 1",
        "cx 0 0", "t 0 0", "rz 3 1", "cd 1 2", "ru 1 0", "cu 2 1", "ru 3 1", "cu 1 2", "ru 2 1", "rz 3 0",
        "rf 1 0", "cu 3 0", "cd 1 1", "ru 1 2", "cd 3 0", "rf 2 0", "rf 1 1", "cd 3 1", "m 1", "t 0 3 0",
        "cd 3 2", "cu 3 2", "rd 2 2", "cu 2 0", "t 0 1", "t 2 0", "rd 3 2", "cx 1 0", "ru 2 2", "ru 3 2",
        "cd 2 2", "cu 3 1", "cx 1 1", "t 0 3 1", "t 1 3 0", "ru 1 1", "m 0", "cu 1 1", "cu 2 2", "cx 2 0",
        "rd 3 1", "t 1 1", "t 1 3 1", "t 2 3 0", "t 3 0", "t 2 2", "rf 3 0", "cx 3 1", "m 2", "rd 3 0",
        "m 5", "t 1 2", "t 3 2", "cx 3 0", "rf 2 1", "t 2 1", "rf 3 1", "cx 2 1", "m 4", "t 3 1", "t 3 3 0",
        "m 3", "t 2 3 1", "t 3 3 1", "m 6",
    )
)


def of_row(px, i):
    if i == 2:
        return [("rz", px, 0), ("rz", px, 1)]
    return [] if (px, i) == (0, 0) else [("r", px, i)]


def of_column(py, i):
    if i == 0:
        return [("c", py, ok, 0) for ok in range(2) if (py, ok) != (0, 0)]
    return [("z1", py)] if i == 1 else [("z2", py), ("z3", py)]


def row_half(px, py, q):
    if py == 0:
        return [n for i in PARTS_OF[q] for n in of_row(px, i)]
    if py == 3:
        return [("rf", px, q)]
    return [("rd" if py == 1 else "ru", px, i) for i in PARTS_OF[q]]


def column_half(px, py, q):
    if px == 0:
        return [n for i in PARTS_OF[q] for n in of_column(py, i)]
    if px == 3:
        return [("cx", py, q)]
    return [("cd" if px == 1 else "cu", py, i) for i in PARTS_OF[q]]


def product_needs(parts):
    out = ["k3"]
    for px, py, e, n in parts:
        for q in range(2):
            if e <= 2 * q < e + n:
                out += row_half(px, py, q) + column_half(px, py, q)
                out.append(("t", px, py, q) if py == 3 else ("t", px, py))
    return out


def over_rows(left, right):
    return lax.dot_general(
        left, right, (((0,), (0,)), ((), ())), preferred_element_type=jnp.float32
    )


def at_group(px, py):
    return px * 4 + py


def rows_of(ref, parts, lanes):
    out = [ref[at_group(px, py), :, pl.ds(e, n), :, lanes] for px, py, e, n in parts]
    return jnp.concatenate([p.reshape(-1, p.shape[-1]) for p in out], axis=0)


def exchange(
    x_hbm, lab_hbm, val_hbm, cw_hbm, acc, sums, rp, last, cp, tb, sc, xs, codes, lab_ref, val_ref, cw_ref, send, recv, local
):
    tok, width = x_hbm.shape
    block = width // 8
    half = block // 2
    row, col = lax.axis_index("row"), lax.axis_index("col")
    x, zh = row // 2, row % 2
    zl, y, core = col // 8, (col // 2) % 4, col % 2

    def flip(v, by):
        return (1 - v) if by else v

    def device(ox=0, oy=0, ozh=0, ozl=0, ok=0):
        r = ((x + ox) % 4) * 2 + flip(zh, ozh)
        c = (flip(zl, ozl) * 4 + (y + oy) % 4) * 2 + flip(core, ok)
        return r, c

    row_peers = [(p, h) for p in range(4) for h in range(2) if (p, h) != (0, 0)]
    col_peers = [(p, ok) for p in range(4) for ok in range(2) if (p, ok) != (0, 0)]
    peers = (
        [device(ox=OFF[p], ozh=h, ozl=h) for p, h in row_peers]
        + [device(oy=OFF[p], ok=ok) for p, ok in col_peers]
        + [device(ozl=1), device(ozh=1)]
    )
    barrier = pltpu.get_barrier_semaphore()
    for peer in peers:
        pl.semaphore_signal(barrier, inc=1, device_id=peer, device_id_type=MESH)

    stage = pltpu.make_async_copy(x_hbm, xs, local.at[6])

    def row_block(src, r):
        return src.at[:, pl.ds(pl.multiple_of(r * block, block), block)]

    def col_block(src, zl, y, core):
        return src.at[:, pl.ds(pl.multiple_of(((zl * 4 + y) * 2 + core) * half, half), half)]

    own = [
        pltpu.make_async_copy(s, d, local.at[i])
        for i, (s, d) in enumerate(
            (
                (lab_hbm, lab_ref),
                (val_hbm, val_ref),
                (cw_hbm, cw_ref),
                (row_block(x_hbm, row), rp.at[0, 0, 0]),
                (col_block(x_hbm, zl, y, core), cp.at[0, 0, 0]),
                (col_block(x_hbm, 1 - zl, y, core), tb.at[0, 0]),
            )
        )
    ]
    for s in own:
        s.start()
    for s in own[:2]:
        s.wait()
    codes[0, 0, 0, 0] = jnp.zeros((1, 128), jnp.float32)
    codes[0, 0, 0, 0, :, :tok] = (val_ref[...] * (lab_ref[...] + 1) - 1).astype(jnp.float32)
    for s in own[2:]:
        s.wait()
    pl.semaphore_wait(barrier, len(peers))

    copies = {}

    def go(name, src, dst, to):
        i = len(copies)
        copies[name] = pltpu.make_async_remote_copy(
            src_ref=src,
            dst_ref=dst,
            send_sem=send.at[i],
            recv_sem=recv.at[i],
            device_id=to,
            device_id_type=MESH,
        )
        copies[name].start()

    seen = set()

    def got(names):
        for n in names:
            if n not in seen:
                seen.add(n)
                copies[n].wait_recv()

    def r_at(px, py, part):
        return rp.at[at_group(px, py), 0, pl.ds(*part)]

    def c_at(px, py, part):
        return cp.at[at_group(px, py), :, pl.ds(*part)]

    def r_at(px, py, part):
        return rp.at[at_group(px, py), 0, pl.ds(*part)]

    def c_at(px, py, part):
        return cp.at[at_group(px, py), :, pl.ds(*part)]

    def step(kind, *at):
        name = (kind, *at)
        if kind == "r":
            px, h = at
            to = device(ox=OFF[NEG[px]], ozh=h, ozl=h)
            go(name, row_block(x_hbm, to[0]), rp.at[at_group(px, 0), 0, h], to)
        elif kind == "c":
            py, ok, other = at
            oy = OFF[NEG[py]]
            src = col_block(x_hbm, flip(zl, other), (y + oy) % 4, flip(core, ok))
            dst = tb.at[py, ok] if other else cp.at[at_group(0, py), ok, 0]
            go(name, src, dst, device(oy=oy, ok=ok))
        elif kind == "rz":
            px, h = at
            got(of_row(px, h))
            go(name, r_at(px, 0, (h, 1)), r_at(px, 0, (2 + h, 1)), device(ozl=1))
        elif kind in ("z1", "z2"):
            (py,) = at
            got([("c", py, ok, 1) for ok in range(2) if (py, ok) != (0, 0)])
            e = 1 if kind == "z1" else 2
            go(name, tb.at[py], cp.at[at_group(0, py), :, e], device(ozl=1, ozh=2 - e))
        elif kind == "z3":
            g = at_group(0, at[0])
            got(of_column(at[0], 0))
            go(name, cp.at[g, :, 0], cp.at[g, :, 3], device(ozh=1))
        elif kind in ("ru", "rd"):
            px, i = at
            got(of_row(px, i))
            py, oy = (2, 1) if kind == "ru" else (1, 3)
            go(name, r_at(px, 0, PARTS[i]), r_at(px, py, PARTS[i]), device(oy=oy))
        elif kind in ("cu", "cd"):
            py, i = at
            got(of_column(py, i))
            px, ox = (2, 1) if kind == "cu" else (1, 3)
            go(name, c_at(0, py, PARTS[i]), c_at(px, py, PARTS[i]), device(ox=ox))
        elif kind == "rf":
            px, q = at
            py, oy = (2, 1) if px in UPWARD else (1, 3)
            got(row_half(px, py, q))
            go(name, r_at(px, py, HALVES[q]), r_at(px, 3, HALVES[q]), device(oy=oy))
        elif kind == "cx":
            py, q = at
            px, ox = (2, 1) if py in UPWARD else (1, 3)
            got(column_half(px, py, q))
            go(name, c_at(px, py, HALVES[q]), c_at(3, py, HALVES[q]), device(ox=ox))
        elif kind == "t":
            px, py = at[:2]
            for q in at[2:] or range(2):
                got(row_half(px, py, q))
            part = pl.ds(*(HALVES[at[2]] if at[2:] else (0, 4)))
            g = at_group(px, py)
            go(name, rp.at[g, 0, part], rp.at[g, 1, part], device(ok=1))
        elif kind == "k1":
            for p, h in row_peers:
                to = device(ox=OFF[NEG[p]], ozh=h, ozl=h)
                go(("k1", p, h), codes.at[0, 0, 0, 0], codes.at[p, 0, 0, h], to)
        elif kind == "k2":
            got([("k1", p, h) for p, h in row_peers])
            for p, ok in col_peers:
                two = pl.ds(0, 2)
                to = device(oy=OFF[NEG[p]], ok=ok)
                go(("k2", p, ok), codes.at[:, 0, 0, two], codes.at[:, p, ok, two], to)
        elif kind == "k3":
            got([("k2", p, ok) for p, ok in col_peers])
            src, dst = (codes.at[:, :, :, pl.ds(e, 2)] for e in (0, 2))
            go("k3", src, dst, device(ozl=1))
        else:
            got(product_needs(CHUNKS[at[0]]))
            multiply(at[0])

    lane = pl.multiple_of(col * 128, 128)
    pick = lax.broadcasted_iota(jnp.int32, (8 * tok, 128), 1) == lax.broadcasted_iota(
        jnp.int32, (8 * tok, 128), 0
    ) % tok
    lanes = lax.broadcasted_iota(jnp.int32, (8 * tok, 128), 1).astype(jnp.float32)

    def weigh(parts, into):
        rows = [
            jnp.broadcast_to(codes[px, py, k, e + i], (tok, 128))
            for px, py, e, n in parts
            for k in range(2)
            for i in range(n)
        ]
        kept = []
        for a in range(0, len(rows), 8):
            spread = jnp.concatenate(rows[a : a + 8], axis=0)
            code = jnp.sum(jnp.where(pick, spread, 0.0), axis=1, keepdims=True)
            kept.append((lanes == code).astype(jnp.float32))
        kept = jnp.concatenate(kept, axis=0)
        w = jnp.sum(kept[:, :64] * cw_ref[...], axis=1, keepdims=True)
        into[...] = (w * rows_of(cp, parts, slice(None)).astype(jnp.float32)).astype(jnp.bfloat16)
        mine = rows_of(rp, parts, pl.ds(lane, 128))
        both = jnp.concatenate([mine, jnp.ones(mine.shape, jnp.bfloat16)], axis=1)
        return over_rows(kept.astype(jnp.bfloat16), both)

    def multiply(n):
        first = ("m",) not in seen
        seen.add(("m",))
        part = weigh(CHUNKS[n], sc)
        if first:
            sums[...] = part
        else:
            sums[...] += part

        @pl.loop(0, 2)
        def _(i):
            at = pl.ds(pl.multiple_of(i * half, half), half)
            left = rows_of(rp, CHUNKS[n], at)
            for j in range(half // 256):
                to = pl.ds(j * 256, 256)
                part = over_rows(left, sc[:, to])
                if first:
                    acc[at, to] = part
                else:
                    acc[at, to] += part

    for one in ORDER:
        step(*one)
    got(product_needs(LAST))
    sums[...] += weigh(LAST, last)
    for c in copies.values():
        c.wait_send()


def finish(acc, sums, rp, last, gram_hbm, means_hbm, out, means, sems):
    rows, half = acc.shape
    total = 16 * 8 * rp.shape[3]
    means[...] = sums[:64, :128] / (sums[:64, 128:] + 1.0)
    writes = [pltpu.make_async_copy(means, means_hbm, sems.at[0])]
    writes[0].start()
    for i in range(2):
        at = pl.ds(i * half, half)
        left = rows_of(rp, LAST, at)
        for j in range(half // 256):
            to = pl.ds(j * 256, 256)
            out[at, to] = (acc[at, to] + over_rows(left, last[:, to])) / float(total)
            n = len(writes)
            writes.append(pltpu.make_async_copy(out.at[at, to], gram_hbm.at[at, to], sems.at[n]))
            writes[n].start()
    for w in writes:
        w.wait()


def body(activations, labels, valid, class_weight):
    tok, width = activations.shape
    classes = class_weight.shape[0]
    block = width // 8
    half = block // 2
    chunk = 2 * 8 * tok
    vmem = pl.BlockSpec(memory_space=pltpu.VMEM)
    hbm = pl.BlockSpec(memory_space=pltpu.HBM)
    parts = pl.pallas_call(
        exchange,
        out_shape=(
            pltpu.VMEM((block, half), jnp.float32),
            pltpu.VMEM((128, 256), jnp.float32),
            pltpu.VMEM((16, 2, 4, tok, block), jnp.bfloat16),
            pltpu.VMEM((chunk, half), jnp.bfloat16),
        ),
        in_specs=[hbm] * 4,
        out_specs=(vmem,) * 4,
        scratch_shapes=[
            pltpu.VMEM((16, 2, 4, tok, half), jnp.bfloat16),
            pltpu.VMEM((4, 2, tok, half), jnp.bfloat16),
            pltpu.VMEM((chunk, half), jnp.bfloat16),
            pltpu.VMEM((tok, width), jnp.bfloat16),
            pltpu.VMEM((4, 4, 2, 4, 1, 128), jnp.float32),
            pltpu.VMEM((1, tok), jnp.int32),
            pltpu.VMEM((1, tok), jnp.int32),
            pltpu.VMEM((1, classes), jnp.float32),
            pltpu.SemaphoreType.DMA((160,)),
            pltpu.SemaphoreType.DMA((160,)),
            pltpu.SemaphoreType.DMA((7,)),
        ],
        compiler_params=pltpu.CompilerParams(
            collective_id=0, has_side_effects=True, vmem_limit_bytes=12 * 1024 * 1024
        ),
    )(
        *[
            pltpu.with_memory_space_constraint(a, pltpu.HBM)
            for a in (
                activations,
                labels.reshape(1, tok),
                valid.reshape(1, tok),
                class_weight.reshape(1, classes),
            )
        ]
    )
    return pl.pallas_call(
        finish,
        out_shape=(
            jax.ShapeDtypeStruct((block, half), jnp.float32),
            jax.ShapeDtypeStruct((classes, 128), jnp.float32),
        ),
        in_specs=[vmem] * 4,
        out_specs=(hbm, hbm),
        scratch_shapes=[
            pltpu.VMEM((block, half), jnp.float32),
            pltpu.VMEM((classes, 128), jnp.float32),
            pltpu.SemaphoreType.DMA((9,)),
        ],
        compiler_params=pltpu.CompilerParams(vmem_limit_bytes=14 * 1024 * 1024),
    )(*parts)


def solution(mesh):
    in_specs = (P(("row", "col"), None), P(("row", "col")), P(("row", "col")), P())
    out_specs = (P("row", "col"), P(None, ("row", "col")))
    return jax.shard_map(body, mesh=mesh, in_specs=in_specs, out_specs=out_specs, check_vma=False)
```

```python
import jax
import jax.numpy as jnp
from jax import lax
from jax.experimental import pallas as pl
from jax.experimental.pallas import tpu as pltpu
from jax.sharding import PartitionSpec as P

MESH = pl.DeviceIdType.MESH

OFF = (0, 1, 3, 2)
NEG = (0, 2, 1, 3)
UPWARD = (0, 3)
PARTS = ((0, 1), (1, 1), (2, 2))
HALVES = ((0, 2), (2, 2))
PARTS_OF = ((0, 1), (2,))
ROW_LATER = ()
COLUMN_LATER = ()
CHUNKS = (
    ((0, 0, 0, 4), (0, 1, 0, 4)),
    ((0, 2, 0, 4), (1, 0, 0, 4)),
    ((2, 0, 0, 4), (1, 1, 0, 4)),
    ((1, 2, 0, 4), (2, 1, 0, 4)),
    ((2, 2, 0, 4), (0, 3, 0, 4)),
    ((3, 0, 0, 4), (1, 3, 0, 4)),
    ((3, 1, 0, 4), (2, 3, 0, 2), (3, 2, 0, 2)),
)
LAST = ((3, 3, 0, 4), (2, 3, 2, 2), (3, 2, 2, 2))


KINDS = range(22)
R, C, RZ, Z1, Z2, Z3, RU, RD, CU, CD, RF, CX, RV, T, K1, K2, K3, S2, M, OWN, READY, FAR = KINDS
ORDER = (
    (C, 0, 1, 1), (C, 0, 1, 0), (C, 1, 0, 1), (C, 1, 0, 0), (RZ, 0, 0), (R, 1, 0), (R, 0, 1), (C, 2, 0, 0),
    (C, 2, 0, 1), (R, 2, 0), (RU, 0, 0), (RD, 0, 0), (S2,), (C, 3, 1, 1), (C, 2, 1, 1), (R, 1, 1),
    (C, 3, 0, 0), (K1,), (CU, 0, 0), (Z3, 0), (Z2, 0), (C, 1, 1, 0), (Z1, 0), (C, 3, 1, 0), (R, 3, 0),
    (R, 3, 1), (C, 2, 1, 0), (C, 1, 1, 1), (R, 2, 1), (RU, 0, 1), (RD, 1, 0), (RZ, 0, 1), (RD, 1, 1),
    (CD, 1, 0), (Z1, 2), (RU, 2, 0), (RZ, 1, 0), (RZ, 1, 1), (CU, 0, 2), (C, 3, 0, 1), (K2,), (RD, 2, 0),
    (CD, 0, 0), (RU, 3, 0), (CU, 0, 1), (CD, 0, 2), (Z2, 1), (RD, 0, 1), (CD, 0, 1), (RU, 0, 2), (Z3, 1),
    (Z1, 1), (CD, 2, 0), (CD, 2, 1), (CU, 1, 0), (RD, 1, 2), (RD, 2, 1), (RF, 0, 0), (Z3, 3), (Z2, 2),
    (RZ, 2, 1), (T, 1, 0), (Z3, 2), (CX, 0, 1), (T, 0, 2), (K3,), (Z2, 3), (Z1, 3), (RD, 0, 2), (RZ, 2, 0),
    (RF, 0, 1), (CX, 0, 0), (T, 0, 0), (RZ, 3, 1), (CD, 1, 2), (RU, 1, 0), (CU, 2, 1), (RU, 3, 1),
    (CU, 1, 2), (RU, 2, 1), (RZ, 3, 0), (RF, 1, 0), (CU, 3, 0), (CD, 1, 1), (RU, 1, 2), (CD, 3, 0),
    (RF, 2, 0), (RF, 1, 1), (CD, 3, 1), (M, 1), (T, 0, 3, 0), (CD, 3, 2), (CU, 3, 2), (RD, 2, 2),
    (CU, 2, 0), (T, 0, 1), (T, 2, 0), (RD, 3, 2), (CX, 1, 0), (RU, 2, 2), (RU, 3, 2), (CD, 2, 2),
    (CU, 3, 1), (CX, 1, 1), (T, 0, 3, 1), (T, 1, 3, 0), (RU, 1, 1), (M, 0), (CU, 1, 1), (CU, 2, 2),
    (CX, 2, 0), (RD, 3, 1), (T, 1, 1), (T, 1, 3, 1), (T, 2, 3, 0), (T, 3, 0), (T, 2, 2), (RF, 3, 0),
    (CX, 3, 1), (M, 2), (RD, 3, 0), (M, 5), (T, 1, 2), (T, 3, 2), (CX, 3, 0), (RF, 2, 1), (T, 2, 1),
    (RF, 3, 1), (CX, 2, 1), (M, 4), (T, 3, 1), (T, 3, 3, 0), (M, 3), (T, 2, 3, 1), (T, 3, 3, 1), (M, 6),
)


def row_ready(px, h):
    if px == 3:
        return [(FAR, "next") if h else (READY, "x+")]
    return [(READY, "next")] if px and h else []


def column_ready(py, ok):
    if py == 3:
        return [(FAR, "twin") if ok else (READY, "y+")]
    return [(READY, "twin")] if py and ok else []


def first_of_column(py, other):
    own = [(OWN, 4 + other)] if py == 0 else []
    return own + [(C, py, ok, other) for ok in range(2) if (py, ok) != (0, 0)]


def of_row(px, i):
    if i == 2:
        return [(RV, px, 0)] if px in ROW_LATER else [(RZ, px, 0), (RZ, px, 1)]
    return [(OWN, 3)] if (px, i) == (0, 0) else [(R, px, i)]


def of_column(py, i):
    if i == 0:
        return first_of_column(py, 0)
    return [(Z1, py)] if i == 1 else [(Z2, py)] + ([] if py in COLUMN_LATER else [(Z3, py)])


def row_half(px, py, q):
    if px in ROW_LATER and q == 1:
        return [(RV, px, py)]
    if py == 0:
        return [n for i in PARTS_OF[q] for n in of_row(px, i)]
    if py == 3:
        return [(RF, px, q)]
    return [(RD if py == 1 else RU, px, i) for i in PARTS_OF[q]]


def column_ring(px, py, parts, q):
    if px == 0:
        return [n for i in parts for n in of_column(py, i)]
    if px == 3:
        return [(CX, py, q)]
    return [(CD if px == 1 else CU, py, i) for i in parts]


def column_half(px, py, q):
    later = [(Z3, py, px)] if py in COLUMN_LATER and q == 1 else []
    return column_ring(px, py, PARTS_OF[q], q) + later


def product_needs(parts):
    out = [(K3,)]
    for px, py, e, n in parts:
        for q in range(2):
            if e <= 2 * q < e + n:
                out += row_half(px, py, q) + column_half(px, py, q)
                out.append((T, px, py, q) if py == 3 else (T, px, py))
    return out


def column_part(py, i):
    return (2, 1) if py in COLUMN_LATER and i == 2 else PARTS[i]


def over_rows(left, right):
    return lax.dot_general(
        left, right, (((0,), (0,)), ((), ())), preferred_element_type=jnp.float32
    )


def at_group(px, py):
    return px * 4 + py


def rows_of(ref, parts, lanes):
    out = [ref[at_group(px, py), :, pl.ds(e, n), :, lanes] for px, py, e, n in parts]
    return jnp.concatenate([p.reshape(-1, p.shape[-1]) for p in out], axis=0)


def exchange(
    x_hbm, lab_hbm, val_hbm, cw_hbm, acc, sums, rp, last, cp, tb, sc, codes, lab_ref, val_ref, cw_ref, send, recv, local, ready, far
):
    tok, width = x_hbm.shape
    block = width // 8
    half = block // 2
    row, col = lax.axis_index("row"), lax.axis_index("col")
    x, zh = row // 2, row % 2
    zl, y, core = col // 8, (col // 2) % 4, col % 2

    def flip(v, by):
        return (1 - v) if by else v

    def device(ox=0, oy=0, ozh=0, ozl=0, ok=0):
        r = ((x + ox) % 4) * 2 + flip(zh, ozh)
        c = (flip(zl, ozl) * 4 + (y + oy) % 4) * 2 + flip(core, ok)
        return r, c

    row_peers = [(p, h) for p in range(4) for h in range(2) if (p, h) != (0, 0)]
    col_peers = [(p, ok) for p in range(4) for ok in range(2) if (p, ok) != (0, 0)]
    near = {
        "x+": dict(ox=1),
        "x-": dict(ox=3),
        "y+": dict(oy=1),
        "y-": dict(oy=3),
        "pair": dict(ozl=1),
        "next": dict(ozl=1, ozh=1),
        "twin": dict(ok=1),
    }
    sides = list(near)
    mirror = {"x+": "x-", "x-": "x+", "y+": "y-", "y-": "y+"}
    barrier = pltpu.get_barrier_semaphore()
    for to in near.values():
        pl.semaphore_signal(barrier, inc=1, device_id=device(**to), device_id_type=MESH)

    def tell(sems, d):
        sem = sems.at[sides.index(mirror.get(d, d))]
        pl.semaphore_signal(sem, inc=1, device_id=device(**near[d]), device_id_type=MESH)

    def row_block(r):
        return x_hbm.at[:, pl.ds(pl.multiple_of(r * block, block), block)]

    def col_block(zl, y, core):
        return x_hbm.at[:, pl.ds(pl.multiple_of(((zl * 4 + y) * 2 + core) * half, half), half)]

    own = [
        pltpu.make_async_copy(s, d, local.at[i])
        for i, (s, d) in enumerate(
            (
                (lab_hbm, lab_ref),
                (val_hbm, val_ref),
                (cw_hbm, cw_ref),
                (row_block(row), rp.at[0, 0, 0]),
                (col_block(zl, y, core), cp.at[0, 0, 0]),
                (col_block(1 - zl, y, core), tb.at[0, 0]),
            )
        )
    ]
    for s in own:
        s.start()
    pl.semaphore_wait(barrier, len(near))
    for d in near:
        tell(ready, d)

    copies = {}

    def go(name, src, dst, to):
        i = len(copies)
        copies[name] = pltpu.make_async_remote_copy(
            src_ref=src,
            dst_ref=dst,
            send_sem=send.at[i],
            recv_sem=recv.at[i],
            device_id=to,
            device_id_type=MESH,
        )
        copies[name].start()

    seen = set()

    def got(names):
        for n in names:
            if n not in seen:
                seen.add(n)
                if n[0] == OWN:
                    own[n[1]].wait()
                elif n[0] in (READY, FAR):
                    sems = ready if n[0] == READY else far
                    pl.semaphore_wait(sems.at[sides.index(n[1])], 1)
                else:
                    copies[n].wait_recv()

    def r_at(px, py, part):
        return rp.at[at_group(px, py), 0, pl.ds(*part)]

    def c_at(px, py, part):
        return cp.at[at_group(px, py), :, pl.ds(*part)]

    def r_at(px, py, part):
        return rp.at[at_group(px, py), 0, pl.ds(*part)]

    def c_at(px, py, part):
        return cp.at[at_group(px, py), :, pl.ds(*part)]

    def step(kind, *at):
        name = (kind, *at)
        if kind == R:
            px, h = at
            got(row_ready(px, h))
            to = device(ox=OFF[NEG[px]], ozh=h, ozl=h)
            go(name, row_block(to[0]), rp.at[at_group(px, 0), 0, h], to)
        elif kind == C:
            py, ok, other = at
            got(column_ready(py, ok))
            oy = OFF[NEG[py]]
            src = col_block(flip(zl, other), (y + oy) % 4, flip(core, ok))
            dst = tb.at[py, ok] if other else cp.at[at_group(0, py), ok, 0]
            go(name, src, dst, device(oy=oy, ok=ok))
        elif kind == RZ:
            px, h = at
            got(of_row(px, h))
            go(name, r_at(px, 0, (h, 1)), r_at(px, 0, (2 + h, 1)), device(ozl=1))
        elif kind == RV:
            px, py = at
            got(row_half(px, py, 0))
            go(name, r_at(px, py, HALVES[0]), r_at(px, py, HALVES[1]), device(ozl=1))
        elif kind in (Z1, Z2):
            (py,) = at
            got(first_of_column(py, 1))
            e = 1 if kind == Z1 else 2
            go(name, tb.at[py], cp.at[at_group(0, py), :, e], device(ozl=1, ozh=2 - e))
        elif kind == Z3:
            py, px = at if len(at) == 2 else (at[0], 0)
            g = at_group(px, py)
            got(column_ring(px, py, (0,), 0) + [(READY, "next")])
            go(name, cp.at[g, :, 0], cp.at[g, :, 3], device(ozh=1))
        elif kind in (RU, RD):
            px, i = at
            got(of_row(px, i))
            py, oy = (2, 1) if kind == RU else (1, 3)
            go(name, r_at(px, 0, PARTS[i]), r_at(px, py, PARTS[i]), device(oy=oy))
        elif kind in (CU, CD):
            py, i = at
            got(of_column(py, i))
            px, ox = (2, 1) if kind == CU else (1, 3)
            part = column_part(py, i)
            go(name, c_at(0, py, part), c_at(px, py, part), device(ox=ox))
        elif kind == RF:
            px, q = at
            py, oy = (2, 1) if px in UPWARD else (1, 3)
            got(row_half(px, py, q))
            go(name, r_at(px, py, HALVES[q]), r_at(px, 3, HALVES[q]), device(oy=oy))
        elif kind == CX:
            py, q = at
            px, ox = (2, 1) if py in UPWARD else (1, 3)
            got(column_ring(px, py, PARTS_OF[q], q))
            part = column_part(py, 2) if q else HALVES[0]
            go(name, c_at(px, py, part), c_at(3, py, part), device(ox=ox))
        elif kind == T:
            px, py = at[:2]
            for q in at[2:] or range(2):
                got(row_half(px, py, q))
            part = pl.ds(*(HALVES[at[2]] if at[2:] else (0, 4)))
            g = at_group(px, py)
            go(name, rp.at[g, 0, part], rp.at[g, 1, part], device(ok=1))
        elif kind == S2:
            got([(READY, "x+"), (READY, "y+")])
            tell(far, "next")
            tell(far, "twin")
        elif kind == K1:
            got([(OWN, 0), (OWN, 1)])
            codes[0, 0, 0, 0] = jnp.zeros((1, 128), jnp.float32)
            codes[0, 0, 0, 0, :, :tok] = (val_ref[...] * (lab_ref[...] + 1) - 1).astype(jnp.float32)
            for p, h in row_peers:
                got(row_ready(p, h))
                to = device(ox=OFF[NEG[p]], ozh=h, ozl=h)
                go((K1, p, h), codes.at[0, 0, 0, 0], codes.at[p, 0, 0, h], to)
        elif kind == K2:
            got([(K1, p, h) for p, h in row_peers])
            for p, ok in col_peers:
                got(column_ready(p, ok))
                two = pl.ds(0, 2)
                to = device(oy=OFF[NEG[p]], ok=ok)
                go((K2, p, ok), codes.at[:, 0, 0, two], codes.at[:, p, ok, two], to)
        elif kind == K3:
            got([(K2, p, ok) for p, ok in col_peers])
            src, dst = (codes.at[:, :, :, pl.ds(e, 2)] for e in (0, 2))
            go(name, src, dst, device(ozl=1))
        else:
            got(product_needs(CHUNKS[at[0]]))
            multiply(at[0])

    lane = pl.multiple_of(col * 128, 128)
    pick = lax.broadcasted_iota(jnp.int32, (8 * tok, 128), 1) == lax.broadcasted_iota(
        jnp.int32, (8 * tok, 128), 0
    ) % tok
    lanes = lax.broadcasted_iota(jnp.int32, (8 * tok, 128), 1).astype(jnp.float32)

    def weigh(parts, into):
        got([(OWN, 2)])
        rows = [
            jnp.broadcast_to(codes[px, py, k, e + i], (tok, 128))
            for px, py, e, n in parts
            for k in range(2)
            for i in range(n)
        ]
        kept = []
        for a in range(0, len(rows), 8):
            spread = jnp.concatenate(rows[a : a + 8], axis=0)
            code = jnp.sum(jnp.where(pick, spread, 0.0), axis=1, keepdims=True)
            kept.append((lanes == code).astype(jnp.float32))
        kept = jnp.concatenate(kept, axis=0)
        w = jnp.sum(kept[:, :64] * cw_ref[...], axis=1, keepdims=True)
        into[...] = (w * rows_of(cp, parts, slice(None)).astype(jnp.float32)).astype(jnp.bfloat16)
        mine = rows_of(rp, parts, pl.ds(lane, 128))
        both = jnp.concatenate([mine, jnp.ones(mine.shape, jnp.bfloat16)], axis=1)
        return over_rows(kept.astype(jnp.bfloat16), both)

    def multiply(n):
        first = (M,) not in seen
        seen.add((M,))
        part = weigh(CHUNKS[n], sc)
        if first:
            sums[...] = part
        else:
            sums[...] += part

        @pl.loop(0, 2)
        def _(i):
            at = pl.ds(pl.multiple_of(i * half, half), half)
            left = rows_of(rp, CHUNKS[n], at)
            for j in range(half // 256):
                to = pl.ds(j * 256, 256)
                part = over_rows(left, sc[:, to])
                if first:
                    acc[at, to] = part
                else:
                    acc[at, to] += part

    for one in ORDER:
        step(*one)
    got(product_needs(LAST) + [(READY, d) for d in near])
    sums[...] += weigh(LAST, last)
    for c in copies.values():
        c.wait_send()


def finish(acc, sums, rp, last, gram_hbm, means_hbm, out, means, sems):
    rows, half = acc.shape
    total = 16 * 8 * rp.shape[3]
    means[...] = sums[:64, :128] / (sums[:64, 128:] + 1.0)
    writes = [pltpu.make_async_copy(means, means_hbm, sems.at[0])]
    writes[0].start()
    for i in range(2):
        at = pl.ds(i * half, half)
        left = rows_of(rp, LAST, at)
        for j in range(half // 256):
            to = pl.ds(j * 256, 256)
            out[at, to] = (acc[at, to] + over_rows(left, last[:, to])) / float(total)
            n = len(writes)
            writes.append(pltpu.make_async_copy(out.at[at, to], gram_hbm.at[at, to], sems.at[n]))
            writes[n].start()
    for w in writes:
        w.wait()


def body(activations, labels, valid, class_weight):
    tok, width = activations.shape
    classes = class_weight.shape[0]
    block = width // 8
    half = block // 2
    chunk = 2 * 8 * tok
    vmem = pl.BlockSpec(memory_space=pltpu.VMEM)
    hbm = pl.BlockSpec(memory_space=pltpu.HBM)
    parts = pl.pallas_call(
        exchange,
        out_shape=(
            pltpu.VMEM((block, half), jnp.float32),
            pltpu.VMEM((128, 256), jnp.float32),
            pltpu.VMEM((16, 2, 4, tok, block), jnp.bfloat16),
            pltpu.VMEM((chunk, half), jnp.bfloat16),
        ),
        in_specs=[hbm] * 4,
        out_specs=(vmem,) * 4,
        scratch_shapes=[
            pltpu.VMEM((16, 2, 4, tok, half), jnp.bfloat16),
            pltpu.VMEM((4, 2, tok, half), jnp.bfloat16),
            pltpu.VMEM((chunk, half), jnp.bfloat16),
            pltpu.VMEM((4, 4, 2, 4, 1, 128), jnp.float32),
            pltpu.VMEM((1, tok), jnp.int32),
            pltpu.VMEM((1, tok), jnp.int32),
            pltpu.VMEM((1, classes), jnp.float32),
            pltpu.SemaphoreType.DMA((160,)),
            pltpu.SemaphoreType.DMA((160,)),
            pltpu.SemaphoreType.DMA((6,)),
            pltpu.SemaphoreType.REGULAR((7,)),
            pltpu.SemaphoreType.REGULAR((7,)),
        ],
        compiler_params=pltpu.CompilerParams(
            collective_id=0, has_side_effects=True, vmem_limit_bytes=12 * 1024 * 1024
        ),
    )(
        *[
            pltpu.with_memory_space_constraint(a, pltpu.HBM)
            for a in (
                activations,
                labels.reshape(1, tok),
                valid.reshape(1, tok),
                class_weight.reshape(1, classes),
            )
        ]
    )
    return pl.pallas_call(
        finish,
        out_shape=(
            jax.ShapeDtypeStruct((block, half), jnp.float32),
            jax.ShapeDtypeStruct((classes, 128), jnp.float32),
        ),
        in_specs=[vmem] * 4,
        out_specs=(hbm, hbm),
        scratch_shapes=[
            pltpu.VMEM((block, half), jnp.float32),
            pltpu.VMEM((classes, 128), jnp.float32),
            pltpu.SemaphoreType.DMA((9,)),
        ],
        compiler_params=pltpu.CompilerParams(vmem_limit_bytes=14 * 1024 * 1024),
    )(*parts)


def solution(mesh):
    in_specs = (P(("row", "col"), None), P(("row", "col")), P(("row", "col")), P())
    out_specs = (P("row", "col"), P(None, ("row", "col")))
    return jax.shard_map(body, mesh=mesh, in_specs=in_specs, out_specs=out_specs, check_vma=False)
```

```python
import jax
import jax.numpy as jnp
from jax import lax
from jax.experimental import pallas as pl
from jax.experimental.pallas import tpu as pltpu
from jax.sharding import PartitionSpec as P

MESH = pl.DeviceIdType.MESH

OFF = (0, 1, 3, 2)
NEG = (0, 2, 1, 3)
UPWARD = (0, 3)
PARTS = ((0, 1), (1, 1), (2, 2))
HALVES = ((0, 2), (2, 2))
PARTS_OF = ((0, 1), (2,))
ROW_LATER = (0,)
COLUMN_LATER = ()
CHUNKS = (
    ((0, 0, 0, 4), (0, 1, 0, 4)),
    ((0, 2, 0, 4), (1, 0, 0, 4)),
    ((2, 0, 0, 4), (1, 1, 0, 4)),
    ((1, 2, 0, 4), (2, 1, 0, 4)),
    ((2, 2, 0, 4), (0, 3, 0, 4)),
    ((3, 0, 0, 4), (1, 3, 0, 4)),
    ((3, 1, 0, 4), (2, 3, 0, 2), (3, 2, 0, 2)),
)
LAST = ((3, 3, 0, 4), (2, 3, 2, 2), (3, 2, 2, 2))


KINDS = range(22)
R, C, RZ, Z1, Z2, Z3, RU, RD, CU, CD, RF, CX, RV, T, K1, K2, K3, S2, M, OWN, READY, FAR = KINDS
ORDER = (
    (C, 1, 0, 1), (R, 1, 0), (R, 0, 1), (C, 0, 1, 0), (R, 2, 0), (C, 0, 1, 1), (C, 1, 0, 0), (RU, 0, 0),
    (C, 2, 0, 0), (C, 2, 1, 0), (C, 1, 1, 0), (C, 1, 1, 1), (RD, 0, 0), (R, 1, 1), (Z3, 0), (S2,),
    (R, 3, 0), (CD, 0, 0), (Z2, 0), (C, 3, 0, 0), (R, 2, 1), (C, 3, 1, 0), (C, 3, 0, 1), (C, 3, 1, 1),
    (C, 2, 0, 1), (RZ, 1, 0), (R, 3, 1), (RU, 1, 0), (Z3, 1), (RZ, 1, 1), (RU, 1, 1), (RD, 2, 0),
    (RD, 0, 1), (CD, 2, 0), (Z1, 1), (CU, 0, 0), (C, 2, 1, 1), (RU, 0, 1), (Z1, 0), (RD, 1, 1), (Z2, 1),
    (K1,), (RV, 0, 0), (RU, 2, 0), (CU, 0, 2), (RD, 3, 0), (RZ, 3, 0), (RD, 2, 1), (RZ, 2, 1), (CD, 0, 2),
    (RZ, 2, 0), (CU, 1, 0), (CD, 1, 0), (CU, 3, 0), (RD, 1, 2), (CD, 1, 2), (Z3, 2), (RU, 1, 2), (CU, 1, 1),
    (RD, 1, 0), (Z1, 2), (RF, 0, 0), (RZ, 3, 1), (Z2, 2), (Z1, 3), (CU, 0, 1), (Z3, 3), (CX, 0, 1),
    (CD, 0, 1), (K2,), (RV, 0, 1), (RU, 3, 0), (RF, 2, 0), (CU, 1, 2), (CD, 1, 1), (CD, 2, 1), (RU, 3, 1),
    (RD, 2, 2), (CU, 2, 1), (CU, 3, 1), (T, 1, 0), (CD, 3, 0), (CX, 1, 1), (T, 1, 1), (RD, 3, 1), (Z2, 3),
    (T, 3, 0), (RU, 3, 2), (T, 1, 2), (T, 2, 0), (RD, 3, 2), (RU, 2, 2), (T, 0, 3, 0), (K3,), (CU, 2, 0),
    (CX, 0, 0), (T, 2, 3, 0), (CD, 2, 2), (CX, 2, 0), (RF, 1, 1), (RV, 0, 2), (RV, 0, 3), (RU, 2, 1),
    (RF, 3, 0), (RF, 1, 0), (T, 0, 0), (CX, 1, 0), (CD, 3, 1), (T, 2, 1), (RF, 2, 1), (RF, 3, 1), (T, 0, 1),
    (T, 3, 2), (CU, 3, 2), (CU, 2, 2), (CD, 3, 2), (CX, 3, 0), (M, 2), (T, 0, 2), (T, 3, 1), (M, 0),
    (T, 1, 3, 1), (T, 2, 2), (CX, 2, 1), (M, 1), (T, 3, 3, 0), (T, 1, 3, 0), (M, 3), (T, 0, 3, 1),
    (CX, 3, 1), (T, 3, 3, 1), (M, 6), (T, 2, 3, 1), (M, 4), (M, 5),
)


def row_ready(px, h):
    if px == 3:
        return [(FAR, "next") if h else (READY, "x+")]
    return [(READY, "next")] if px and h else []


def column_ready(py, ok):
    if py == 3:
        return [(FAR, "twin") if ok else (READY, "y+")]
    return [(READY, "twin")] if py and ok else []


def first_of_column(py, other):
    own = [(OWN, 4 + other)] if py == 0 else []
    return own + [(C, py, ok, other) for ok in range(2) if (py, ok) != (0, 0)]


def of_row(px, i):
    if i == 2:
        return [(RV, px, 0)] if px in ROW_LATER else [(RZ, px, 0), (RZ, px, 1)]
    return [(OWN, 3)] if (px, i) == (0, 0) else [(R, px, i)]


def of_column(py, i):
    if i == 0:
        return first_of_column(py, 0)
    return [(Z1, py)] if i == 1 else [(Z2, py)] + ([] if py in COLUMN_LATER else [(Z3, py)])


def row_half(px, py, q):
    if px in ROW_LATER and q == 1:
        return [(RV, px, py)]
    if py == 0:
        return [n for i in PARTS_OF[q] for n in of_row(px, i)]
    if py == 3:
        return [(RF, px, q)]
    return [(RD if py == 1 else RU, px, i) for i in PARTS_OF[q]]


def column_ring(px, py, parts, q):
    if px == 0:
        return [n for i in parts for n in of_column(py, i)]
    if px == 3:
        return [(CX, py, q)]
    return [(CD if px == 1 else CU, py, i) for i in parts]


def column_half(px, py, q):
    later = [(Z3, py, px)] if py in COLUMN_LATER and q == 1 else []
    return column_ring(px, py, PARTS_OF[q], q) + later


def product_needs(parts):
    out = [(K3,)]
    for px, py, e, n in parts:
        for q in range(2):
            if e <= 2 * q < e + n:
                out += row_half(px, py, q) + column_half(px, py, q)
                out.append((T, px, py, q) if py == 3 else (T, px, py))
    return out


def column_part(py, i):
    return (2, 1) if py in COLUMN_LATER and i == 2 else PARTS[i]


def over_rows(left, right):
    return lax.dot_general(
        left, right, (((0,), (0,)), ((), ())), preferred_element_type=jnp.float32
    )


def at_group(px, py):
    return px * 4 + py


def rows_of(ref, parts, lanes):
    out = [ref[at_group(px, py), :, pl.ds(e, n), :, lanes] for px, py, e, n in parts]
    return jnp.concatenate([p.reshape(-1, p.shape[-1]) for p in out], axis=0)


def exchange(
    x_hbm, lab_hbm, val_hbm, cw_hbm, acc, sums, rp, last, cp, tb, sc, codes, lab_ref, val_ref, cw_ref, send, recv, local, ready, far
):
    tok, width = x_hbm.shape
    block = width // 8
    half = block // 2
    row, col = lax.axis_index("row"), lax.axis_index("col")
    x, zh = row // 2, row % 2
    zl, y, core = col // 8, (col // 2) % 4, col % 2

    def flip(v, by):
        return (1 - v) if by else v

    def device(ox=0, oy=0, ozh=0, ozl=0, ok=0):
        r = ((x + ox) % 4) * 2 + flip(zh, ozh)
        c = (flip(zl, ozl) * 4 + (y + oy) % 4) * 2 + flip(core, ok)
        return r, c

    row_peers = [(p, h) for p in range(4) for h in range(2) if (p, h) != (0, 0)]
    col_peers = [(p, ok) for p in range(4) for ok in range(2) if (p, ok) != (0, 0)]
    near = {
        "x+": dict(ox=1),
        "x-": dict(ox=3),
        "y+": dict(oy=1),
        "y-": dict(oy=3),
        "pair": dict(ozl=1),
        "next": dict(ozl=1, ozh=1),
        "twin": dict(ok=1),
    }
    sides = list(near)
    mirror = {"x+": "x-", "x-": "x+", "y+": "y-", "y-": "y+"}
    barrier = pltpu.get_barrier_semaphore()
    for to in near.values():
        pl.semaphore_signal(barrier, inc=1, device_id=device(**to), device_id_type=MESH)

    def tell(sems, d):
        sem = sems.at[sides.index(mirror.get(d, d))]
        pl.semaphore_signal(sem, inc=1, device_id=device(**near[d]), device_id_type=MESH)

    def row_block(r):
        return x_hbm.at[:, pl.ds(pl.multiple_of(r * block, block), block)]

    def col_block(zl, y, core):
        return x_hbm.at[:, pl.ds(pl.multiple_of(((zl * 4 + y) * 2 + core) * half, half), half)]

    own = [
        pltpu.make_async_copy(s, d, local.at[i])
        for i, (s, d) in enumerate(
            (
                (lab_hbm, lab_ref),
                (val_hbm, val_ref),
                (cw_hbm, cw_ref),
                (row_block(row), rp.at[0, 0, 0]),
                (col_block(zl, y, core), cp.at[0, 0, 0]),
                (col_block(1 - zl, y, core), tb.at[0, 0]),
            )
        )
    ]
    for s in own:
        s.start()
    pl.semaphore_wait(barrier, len(near))
    for d in near:
        tell(ready, d)

    copies = {}

    def go(name, src, dst, to):
        i = len(copies)
        copies[name] = pltpu.make_async_remote_copy(
            src_ref=src,
            dst_ref=dst,
            send_sem=send.at[i],
            recv_sem=recv.at[i],
            device_id=to,
            device_id_type=MESH,
        )
        copies[name].start()

    seen = set()

    def got(names):
        for n in names:
            if n not in seen:
                seen.add(n)
                if n[0] == OWN:
                    own[n[1]].wait()
                elif n[0] in (READY, FAR):
                    sems = ready if n[0] == READY else far
                    pl.semaphore_wait(sems.at[sides.index(n[1])], 1)
                else:
                    copies[n].wait_recv()

    def r_at(px, py, part):
        return rp.at[at_group(px, py), 0, pl.ds(*part)]

    def c_at(px, py, part):
        return cp.at[at_group(px, py), :, pl.ds(*part)]

    def r_at(px, py, part):
        return rp.at[at_group(px, py), 0, pl.ds(*part)]

    def c_at(px, py, part):
        return cp.at[at_group(px, py), :, pl.ds(*part)]

    def step(kind, *at):
        name = (kind, *at)
        if kind == R:
            px, h = at
            got(row_ready(px, h))
            to = device(ox=OFF[NEG[px]], ozh=h, ozl=h)
            go(name, row_block(to[0]), rp.at[at_group(px, 0), 0, h], to)
        elif kind == C:
            py, ok, other = at
            got(column_ready(py, ok))
            oy = OFF[NEG[py]]
            src = col_block(flip(zl, other), (y + oy) % 4, flip(core, ok))
            dst = tb.at[py, ok] if other else cp.at[at_group(0, py), ok, 0]
            go(name, src, dst, device(oy=oy, ok=ok))
        elif kind == RZ:
            px, h = at
            got(of_row(px, h))
            go(name, r_at(px, 0, (h, 1)), r_at(px, 0, (2 + h, 1)), device(ozl=1))
        elif kind == RV:
            px, py = at
            got(row_half(px, py, 0))
            go(name, r_at(px, py, HALVES[0]), r_at(px, py, HALVES[1]), device(ozl=1))
        elif kind in (Z1, Z2):
            (py,) = at
            got(first_of_column(py, 1))
            e = 1 if kind == Z1 else 2
            go(name, tb.at[py], cp.at[at_group(0, py), :, e], device(ozl=1, ozh=2 - e))
        elif kind == Z3:
            py, px = at if len(at) == 2 else (at[0], 0)
            g = at_group(px, py)
            got(column_ring(px, py, (0,), 0) + [(READY, "next")])
            go(name, cp.at[g, :, 0], cp.at[g, :, 3], device(ozh=1))
        elif kind in (RU, RD):
            px, i = at
            got(of_row(px, i))
            py, oy = (2, 1) if kind == RU else (1, 3)
            go(name, r_at(px, 0, PARTS[i]), r_at(px, py, PARTS[i]), device(oy=oy))
        elif kind in (CU, CD):
            py, i = at
            got(of_column(py, i))
            px, ox = (2, 1) if kind == CU else (1, 3)
            part = column_part(py, i)
            go(name, c_at(0, py, part), c_at(px, py, part), device(ox=ox))
        elif kind == RF:
            px, q = at
            py, oy = (2, 1) if px in UPWARD else (1, 3)
            got(row_half(px, py, q))
            go(name, r_at(px, py, HALVES[q]), r_at(px, 3, HALVES[q]), device(oy=oy))
        elif kind == CX:
            py, q = at
            px, ox = (2, 1) if py in UPWARD else (1, 3)
            got(column_ring(px, py, PARTS_OF[q], q))
            part = column_part(py, 2) if q else HALVES[0]
            go(name, c_at(px, py, part), c_at(3, py, part), device(ox=ox))
        elif kind == T:
            px, py = at[:2]
            for q in at[2:] or range(2):
                got(row_half(px, py, q))
            part = pl.ds(*(HALVES[at[2]] if at[2:] else (0, 4)))
            g = at_group(px, py)
            go(name, rp.at[g, 0, part], rp.at[g, 1, part], device(ok=1))
        elif kind == S2:
            got([(READY, "x+"), (READY, "y+")])
            tell(far, "next")
            tell(far, "twin")
        elif kind == K1:
            got([(OWN, 0), (OWN, 1)])
            codes[0, 0, 0, 0] = jnp.zeros((1, 128), jnp.float32)
            codes[0, 0, 0, 0, :, :tok] = (val_ref[...] * (lab_ref[...] + 1) - 1).astype(jnp.float32)
            for p, h in row_peers:
                got(row_ready(p, h))
                to = device(ox=OFF[NEG[p]], ozh=h, ozl=h)
                go((K1, p, h), codes.at[0, 0, 0, 0], codes.at[p, 0, 0, h], to)
        elif kind == K2:
            got([(K1, p, h) for p, h in row_peers])
            for p, ok in col_peers:
                got(column_ready(p, ok))
                two = pl.ds(0, 2)
                to = device(oy=OFF[NEG[p]], ok=ok)
                go((K2, p, ok), codes.at[:, 0, 0, two], codes.at[:, p, ok, two], to)
        elif kind == K3:
            got([(K2, p, ok) for p, ok in col_peers])
            src, dst = (codes.at[:, :, :, pl.ds(e, 2)] for e in (0, 2))
            go(name, src, dst, device(ozl=1))
        else:
            got(product_needs(CHUNKS[at[0]]))
            multiply(at[0])

    lane = pl.multiple_of(col * 128, 128)
    pick = lax.broadcasted_iota(jnp.int32, (8 * tok, 128), 1) == lax.broadcasted_iota(
        jnp.int32, (8 * tok, 128), 0
    ) % tok
    lanes = lax.broadcasted_iota(jnp.int32, (8 * tok, 128), 1).astype(jnp.float32)

    def weigh(parts, into):
        got([(OWN, 2)])
        rows = [
            jnp.broadcast_to(codes[px, py, k, e + i], (tok, 128))
            for px, py, e, n in parts
            for k in range(2)
            for i in range(n)
        ]
        kept = []
        for a in range(0, len(rows), 8):
            spread = jnp.concatenate(rows[a : a + 8], axis=0)
            code = jnp.sum(jnp.where(pick, spread, 0.0), axis=1, keepdims=True)
            kept.append((lanes == code).astype(jnp.float32))
        kept = jnp.concatenate(kept, axis=0)
        w = jnp.sum(kept[:, :64] * cw_ref[...], axis=1, keepdims=True)
        into[...] = (w * rows_of(cp, parts, slice(None)).astype(jnp.float32)).astype(jnp.bfloat16)
        mine = rows_of(rp, parts, pl.ds(lane, 128))
        both = jnp.concatenate([mine, jnp.ones(mine.shape, jnp.bfloat16)], axis=1)
        return over_rows(kept.astype(jnp.bfloat16), both)

    def multiply(n):
        first = (M,) not in seen
        seen.add((M,))
        part = weigh(CHUNKS[n], sc)
        if first:
            sums[...] = part
        else:
            sums[...] += part

        @pl.loop(0, 2)
        def _(i):
            at = pl.ds(pl.multiple_of(i * half, half), half)
            left = rows_of(rp, CHUNKS[n], at)
            for j in range(half // 256):
                to = pl.ds(j * 256, 256)
                part = over_rows(left, sc[:, to])
                if first:
                    acc[at, to] = part
                else:
                    acc[at, to] += part

    for one in ORDER:
        step(*one)
    got(product_needs(LAST) + [(READY, d) for d in near])
    sums[...] += weigh(LAST, last)
    for c in copies.values():
        c.wait_send()


def finish(acc, sums, rp, last, gram_hbm, means_hbm, out, means, sems):
    rows, half = acc.shape
    total = 16 * 8 * rp.shape[3]
    means[...] = sums[:64, :128] / (sums[:64, 128:] + 1.0)
    writes = [pltpu.make_async_copy(means, means_hbm, sems.at[0])]
    writes[0].start()
    for i in range(rows // 256):
        at = pl.ds(i * 256, 256)
        left = rows_of(rp, LAST, at)
        for j in range(half // 1024):
            to = pl.ds(j * 1024, 1024)
            out[at, to] = (acc[at, to] + over_rows(left, last[:, to])) / float(total)
            n = len(writes)
            writes.append(pltpu.make_async_copy(out.at[at, to], gram_hbm.at[at, to], sems.at[n]))
            writes[n].start()
    for w in writes:
        w.wait()


def body(activations, labels, valid, class_weight):
    tok, width = activations.shape
    classes = class_weight.shape[0]
    block = width // 8
    half = block // 2
    chunk = 2 * 8 * tok
    vmem = pl.BlockSpec(memory_space=pltpu.VMEM)
    hbm = pl.BlockSpec(memory_space=pltpu.HBM)
    parts = pl.pallas_call(
        exchange,
        out_shape=(
            pltpu.VMEM((block, half), jnp.float32),
            pltpu.VMEM((128, 256), jnp.float32),
            pltpu.VMEM((16, 2, 4, tok, block), jnp.bfloat16),
            pltpu.VMEM((chunk, half), jnp.bfloat16),
        ),
        in_specs=[hbm] * 4,
        out_specs=(vmem,) * 4,
        scratch_shapes=[
            pltpu.VMEM((16, 2, 4, tok, half), jnp.bfloat16),
            pltpu.VMEM((4, 2, tok, half), jnp.bfloat16),
            pltpu.VMEM((chunk, half), jnp.bfloat16),
            pltpu.VMEM((4, 4, 2, 4, 1, 128), jnp.float32),
            pltpu.VMEM((1, tok), jnp.int32),
            pltpu.VMEM((1, tok), jnp.int32),
            pltpu.VMEM((1, classes), jnp.float32),
            pltpu.SemaphoreType.DMA((160,)),
            pltpu.SemaphoreType.DMA((160,)),
            pltpu.SemaphoreType.DMA((6,)),
            pltpu.SemaphoreType.REGULAR((7,)),
            pltpu.SemaphoreType.REGULAR((7,)),
        ],
        compiler_params=pltpu.CompilerParams(
            collective_id=0, has_side_effects=True, vmem_limit_bytes=12 * 1024 * 1024
        ),
    )(
        *[
            pltpu.with_memory_space_constraint(a, pltpu.HBM)
            for a in (
                activations,
                labels.reshape(1, tok),
                valid.reshape(1, tok),
                class_weight.reshape(1, classes),
            )
        ]
    )
    return pl.pallas_call(
        finish,
        out_shape=(
            jax.ShapeDtypeStruct((block, half), jnp.float32),
            jax.ShapeDtypeStruct((classes, 128), jnp.float32),
        ),
        in_specs=[vmem] * 4,
        out_specs=(hbm, hbm),
        scratch_shapes=[
            pltpu.VMEM((block, half), jnp.float32),
            pltpu.VMEM((classes, 128), jnp.float32),
            pltpu.SemaphoreType.DMA((9,)),
        ],
        compiler_params=pltpu.CompilerParams(vmem_limit_bytes=14 * 1024 * 1024),
    )(*parts)


def solution(mesh):
    in_specs = (P(("row", "col"), None), P(("row", "col")), P(("row", "col")), P())
    out_specs = (P("row", "col"), P(None, ("row", "col")))
    return jax.shard_map(body, mesh=mesh, in_specs=in_specs, out_specs=out_specs, check_vma=False)
```

```python
import jax
import jax.numpy as jnp
from jax import lax
from jax.experimental import pallas as pl
from jax.experimental.pallas import tpu as pltpu
from jax.sharding import PartitionSpec as P

MESH = pl.DeviceIdType.MESH

OFF = (0, 1, 3, 2)
NEG = (0, 2, 1, 3)
UPWARD = (0, 3)
PARTS = ((0, 1), (1, 1), (2, 2))
HALVES = ((0, 2), (2, 2))
PARTS_OF = ((0, 1), (2,))
ROW_LATER = (0,)
COLUMN_LATER = ()
CHUNKS = (
    ((0, 0, 0, 4), (0, 1, 0, 4)),
    ((0, 2, 0, 4), (1, 0, 0, 4)),
    ((2, 0, 0, 4), (1, 1, 0, 4)),
    ((1, 2, 0, 4), (2, 1, 0, 4)),
    ((2, 2, 0, 4), (0, 3, 0, 4)),
    ((3, 0, 0, 4), (1, 3, 0, 4)),
    ((3, 1, 0, 4), (2, 3, 0, 2), (3, 2, 0, 2)),
)
LAST = ((3, 3, 0, 4), (2, 3, 2, 2), (3, 2, 2, 2))


KINDS = range(22)
R, C, RZ, Z1, Z2, Z3, RU, RD, CU, CD, RF, CX, RV, T, K1, K2, K3, S2, M, OWN, READY, FAR = KINDS
ORDER = (
    (C, 0, 1, 1), (C, 1, 0, 1), (R, 1, 0), (R, 0, 1), (R, 2, 0), (C, 0, 1, 0), (RD, 0, 0), (C, 2, 0, 1),
    (C, 2, 1, 0), (C, 1, 0, 0), (S2,), (R, 1, 1), (Z2, 0), (C, 1, 1, 1), (C, 2, 1, 1), (C, 3, 1, 0),
    (RU, 0, 0), (C, 1, 1, 0), (R, 2, 1), (CD, 0, 0), (R, 3, 0), (C, 3, 1, 1), (Z3, 0), (RZ, 1, 0),
    (C, 2, 0, 0), (RU, 1, 0), (K1,), (R, 3, 1), (C, 3, 0, 0), (RZ, 2, 0), (RD, 0, 1), (C, 3, 0, 1), (Z1, 0),
    (RU, 0, 1), (RZ, 1, 1), (RV, 0, 0), (RD, 1, 1), (Z2, 1), (Z1, 1), (Z1, 2), (RU, 1, 1), (RD, 1, 0),
    (CU, 0, 2), (RD, 2, 0), (RU, 3, 0), (CD, 0, 2), (K2,), (RU, 2, 0), (CU, 0, 0), (CU, 1, 0), (Z3, 1),
    (RZ, 2, 1), (RD, 1, 2), (CD, 2, 0), (Z3, 2), (CU, 0, 1), (Z1, 3), (CU, 2, 0), (RV, 0, 1), (RF, 1, 0),
    (CD, 1, 1), (Z2, 2), (RU, 2, 1), (CD, 3, 0), (RD, 2, 1), (RU, 3, 1), (CD, 2, 1), (CD, 1, 0), (CU, 1, 1),
    (RZ, 3, 1), (RU, 1, 2), (CU, 2, 1), (RF, 0, 0), (RZ, 3, 0), (RF, 1, 1), (CX, 0, 1), (CD, 3, 1),
    (T, 2, 0), (RU, 2, 2), (RD, 2, 2), (CU, 3, 1), (CD, 1, 2), (CU, 3, 0), (RF, 3, 0), (Z3, 3), (CX, 0, 0),
    (RD, 3, 1), (K3,), (T, 0, 1), (RD, 3, 0), (Z2, 3), (CX, 2, 0), (T, 1, 1), (RV, 0, 2), (CU, 2, 2),
    (CD, 2, 2), (T, 0, 0), (RV, 0, 3), (CD, 0, 1), (T, 0, 3, 0), (T, 1, 2), (RD, 3, 2), (RU, 3, 2),
    (T, 1, 0), (T, 1, 3, 1), (RF, 2, 0), (CU, 3, 2), (T, 3, 0), (CD, 3, 2), (T, 1, 3, 0), (CU, 1, 2),
    (T, 2, 2), (CX, 1, 0), (RF, 2, 1), (T, 2, 1), (M, 0), (T, 0, 2), (CX, 3, 0), (M, 2), (RF, 3, 1),
    (T, 3, 2), (T, 3, 3, 0), (CX, 1, 1), (CX, 2, 1), (T, 0, 3, 1), (T, 3, 1), (M, 1), (CX, 3, 1),
    (T, 2, 3, 0), (M, 5), (T, 2, 3, 1), (M, 3), (T, 3, 3, 1), (M, 4), (M, 6),
)


def row_ready(px, h):
    if px == 3:
        return [(FAR, "next") if h else (READY, "x+")]
    return [(READY, "next")] if px and h else []


def column_ready(py, ok):
    if py == 3:
        return [(FAR, "twin") if ok else (READY, "y+")]
    return [(READY, "twin")] if py and ok else []


def first_of_column(py, other):
    own = [(OWN, 4 + other)] if py == 0 else []
    return own + [(C, py, ok, other) for ok in range(2) if (py, ok) != (0, 0)]


def of_row(px, i):
    if i == 2:
        return [(RV, px, 0)] if px in ROW_LATER else [(RZ, px, 0), (RZ, px, 1)]
    return [(OWN, 3)] if (px, i) == (0, 0) else [(R, px, i)]


def of_column(py, i):
    if i == 0:
        return first_of_column(py, 0)
    return [(Z1, py)] if i == 1 else [(Z2, py)] + ([] if py in COLUMN_LATER else [(Z3, py)])


def row_half(px, py, q):
    if px in ROW_LATER and q == 1:
        return [(RV, px, py)]
    if py == 0:
        return [n for i in PARTS_OF[q] for n in of_row(px, i)]
    if py == 3:
        return [(RF, px, q)]
    return [(RD if py == 1 else RU, px, i) for i in PARTS_OF[q]]


def column_ring(px, py, parts, q):
    if px == 0:
        return [n for i in parts for n in of_column(py, i)]
    if px == 3:
        return [(CX, py, q)]
    return [(CD if px == 1 else CU, py, i) for i in parts]


def column_half(px, py, q):
    later = [(Z3, py, px)] if py in COLUMN_LATER and q == 1 else []
    return column_ring(px, py, PARTS_OF[q], q) + later


def product_needs(parts):
    out = [(K3,)]
    for px, py, e, n in parts:
        for q in range(2):
            if e <= 2 * q < e + n:
                out += row_half(px, py, q) + column_half(px, py, q)
                out.append((T, px, py, q) if py == 3 else (T, px, py))
    return out


def column_part(py, i):
    return (2, 1) if py in COLUMN_LATER and i == 2 else PARTS[i]


def over_rows(left, right):
    return lax.dot_general(
        left, right, (((0,), (0,)), ((), ())), preferred_element_type=jnp.float32
    )


def at_group(px, py):
    return px * 4 + py


def rows_of(ref, parts, lanes):
    out = [ref[at_group(px, py), :, pl.ds(e, n), :, lanes] for px, py, e, n in parts]
    return jnp.concatenate([p.reshape(-1, p.shape[-1]) for p in out], axis=0)


def exchange(
    x_hbm, lab_hbm, val_hbm, cw_hbm, acc, sums, rp, last, cp, tb, sc, codes, lab_ref, val_ref, cw_ref, send, recv, local, ready, far
):
    tok, width = x_hbm.shape
    block = width // 8
    half = block // 2
    row, col = lax.axis_index("row"), lax.axis_index("col")
    x, zh = row // 2, row % 2
    zl, y, core = col // 8, (col // 2) % 4, col % 2

    def flip(v, by):
        return (1 - v) if by else v

    def device(ox=0, oy=0, ozh=0, ozl=0, ok=0):
        r = ((x + ox) % 4) * 2 + flip(zh, ozh)
        c = (flip(zl, ozl) * 4 + (y + oy) % 4) * 2 + flip(core, ok)
        return r, c

    row_peers = [(p, h) for p in range(4) for h in range(2) if (p, h) != (0, 0)]
    col_peers = [(p, ok) for p in range(4) for ok in range(2) if (p, ok) != (0, 0)]
    near = {
        "x+": dict(ox=1),
        "x-": dict(ox=3),
        "y+": dict(oy=1),
        "y-": dict(oy=3),
        "pair": dict(ozl=1),
        "next": dict(ozl=1, ozh=1),
        "twin": dict(ok=1),
    }
    sides = list(near)
    mirror = {"x+": "x-", "x-": "x+", "y+": "y-", "y-": "y+"}
    barrier = pltpu.get_barrier_semaphore()
    for to in near.values():
        pl.semaphore_signal(barrier, inc=1, device_id=device(**to), device_id_type=MESH)

    def tell(sems, d):
        sem = sems.at[sides.index(mirror.get(d, d))]
        pl.semaphore_signal(sem, inc=1, device_id=device(**near[d]), device_id_type=MESH)

    def row_block(r):
        return x_hbm.at[:, pl.ds(pl.multiple_of(r * block, block), block)]

    def col_block(zl, y, core):
        return x_hbm.at[:, pl.ds(pl.multiple_of(((zl * 4 + y) * 2 + core) * half, half), half)]

    own = [
        pltpu.make_async_copy(s, d, local.at[i])
        for i, (s, d) in enumerate(
            (
                (lab_hbm, lab_ref),
                (val_hbm, val_ref),
                (cw_hbm, cw_ref),
                (row_block(row), rp.at[0, 0, 0]),
                (col_block(zl, y, core), cp.at[0, 0, 0]),
                (col_block(1 - zl, y, core), tb.at[0, 0]),
            )
        )
    ]
    for s in own:
        s.start()
    pl.semaphore_wait(barrier, len(near))
    for d in near:
        tell(ready, d)

    copies = {}

    def go(name, src, dst, to):
        i = len(copies)
        copies[name] = pltpu.make_async_remote_copy(
            src_ref=src,
            dst_ref=dst,
            send_sem=send.at[i],
            recv_sem=recv.at[i],
            device_id=to,
            device_id_type=MESH,
        )
        copies[name].start()

    seen = set()

    def got(names):
        for n in names:
            if n not in seen:
                seen.add(n)
                if n[0] == OWN:
                    own[n[1]].wait()
                elif n[0] in (READY, FAR):
                    sems = ready if n[0] == READY else far
                    pl.semaphore_wait(sems.at[sides.index(n[1])], 1)
                else:
                    copies[n].wait_recv()

    def r_at(px, py, part):
        return rp.at[at_group(px, py), 0, pl.ds(*part)]

    def c_at(px, py, part):
        return cp.at[at_group(px, py), :, pl.ds(*part)]

    def r_at(px, py, part):
        return rp.at[at_group(px, py), 0, pl.ds(*part)]

    def c_at(px, py, part):
        return cp.at[at_group(px, py), :, pl.ds(*part)]

    def step(kind, *at):
        name = (kind, *at)
        if kind == R:
            px, h = at
            got(row_ready(px, h))
            to = device(ox=OFF[NEG[px]], ozh=h, ozl=h)
            go(name, row_block(to[0]), rp.at[at_group(px, 0), 0, h], to)
        elif kind == C:
            py, ok, other = at
            got(column_ready(py, ok))
            oy = OFF[NEG[py]]
            src = col_block(flip(zl, other), (y + oy) % 4, flip(core, ok))
            dst = tb.at[py, ok] if other else cp.at[at_group(0, py), ok, 0]
            go(name, src, dst, device(oy=oy, ok=ok))
        elif kind == RZ:
            px, h = at
            got(of_row(px, h))
            go(name, r_at(px, 0, (h, 1)), r_at(px, 0, (2 + h, 1)), device(ozl=1))
        elif kind == RV:
            px, py = at
            got(row_half(px, py, 0))
            go(name, r_at(px, py, HALVES[0]), r_at(px, py, HALVES[1]), device(ozl=1))
        elif kind in (Z1, Z2):
            (py,) = at
            got(first_of_column(py, 1))
            e = 1 if kind == Z1 else 2
            go(name, tb.at[py], cp.at[at_group(0, py), :, e], device(ozl=1, ozh=2 - e))
        elif kind == Z3:
            py, px = at if len(at) == 2 else (at[0], 0)
            g = at_group(px, py)
            got(column_ring(px, py, (0,), 0) + [(READY, "next")])
            go(name, cp.at[g, :, 0], cp.at[g, :, 3], device(ozh=1))
        elif kind in (RU, RD):
            px, i = at
            got(of_row(px, i))
            py, oy = (2, 1) if kind == RU else (1, 3)
            go(name, r_at(px, 0, PARTS[i]), r_at(px, py, PARTS[i]), device(oy=oy))
        elif kind in (CU, CD):
            py, i = at
            got(of_column(py, i))
            px, ox = (2, 1) if kind == CU else (1, 3)
            part = column_part(py, i)
            go(name, c_at(0, py, part), c_at(px, py, part), device(ox=ox))
        elif kind == RF:
            px, q = at
            py, oy = (2, 1) if px in UPWARD else (1, 3)
            got(row_half(px, py, q))
            go(name, r_at(px, py, HALVES[q]), r_at(px, 3, HALVES[q]), device(oy=oy))
        elif kind == CX:
            py, q = at
            px, ox = (2, 1) if py in UPWARD else (1, 3)
            got(column_ring(px, py, PARTS_OF[q], q))
            part = column_part(py, 2) if q else HALVES[0]
            go(name, c_at(px, py, part), c_at(3, py, part), device(ox=ox))
        elif kind == T:
            px, py = at[:2]
            for q in at[2:] or range(2):
                got(row_half(px, py, q))
            part = pl.ds(*(HALVES[at[2]] if at[2:] else (0, 4)))
            g = at_group(px, py)
            go(name, rp.at[g, 0, part], rp.at[g, 1, part], device(ok=1))
        elif kind == S2:
            got([(READY, "x+"), (READY, "y+")])
            tell(far, "next")
            tell(far, "twin")
        elif kind == K1:
            got([(OWN, 0), (OWN, 1)])
            codes[0, 0, 0, 0] = jnp.zeros((1, 128), jnp.float32)
            codes[0, 0, 0, 0, :, :tok] = (val_ref[...] * (lab_ref[...] + 1) - 1).astype(jnp.float32)
            for p, h in row_peers:
                got(row_ready(p, h))
                to = device(ox=OFF[NEG[p]], ozh=h, ozl=h)
                go((K1, p, h), codes.at[0, 0, 0, 0], codes.at[p, 0, 0, h], to)
        elif kind == K2:
            got([(K1, p, h) for p, h in row_peers])
            for p, ok in col_peers:
                got(column_ready(p, ok))
                two = pl.ds(0, 2)
                to = device(oy=OFF[NEG[p]], ok=ok)
                go((K2, p, ok), codes.at[:, 0, 0, two], codes.at[:, p, ok, two], to)
        elif kind == K3:
            got([(K2, p, ok) for p, ok in col_peers])
            src, dst = (codes.at[:, :, :, pl.ds(e, 2)] for e in (0, 2))
            go(name, src, dst, device(ozl=1))
        else:
            got(product_needs(CHUNKS[at[0]]))
            multiply(at[0])

    lane = pl.multiple_of(col * 128, 128)
    pick = lax.broadcasted_iota(jnp.int32, (8 * tok, 128), 1) == lax.broadcasted_iota(
        jnp.int32, (8 * tok, 128), 0
    ) % tok
    lanes = lax.broadcasted_iota(jnp.int32, (8 * tok, 128), 1).astype(jnp.float32)

    def weigh(parts, into):
        got([(OWN, 2)])
        rows = [
            jnp.broadcast_to(codes[px, py, k, e + i], (tok, 128))
            for px, py, e, n in parts
            for k in range(2)
            for i in range(n)
        ]
        kept = []
        for a in range(0, len(rows), 8):
            spread = jnp.concatenate(rows[a : a + 8], axis=0)
            code = jnp.sum(jnp.where(pick, spread, 0.0), axis=1, keepdims=True)
            kept.append((lanes == code).astype(jnp.float32))
        kept = jnp.concatenate(kept, axis=0)
        w = jnp.sum(kept[:, :64] * cw_ref[...], axis=1, keepdims=True)
        into[...] = (w * rows_of(cp, parts, slice(None)).astype(jnp.float32)).astype(jnp.bfloat16)
        mine = rows_of(rp, parts, pl.ds(lane, 128))
        both = jnp.concatenate([mine, jnp.ones(mine.shape, jnp.bfloat16)], axis=1)
        return over_rows(kept.astype(jnp.bfloat16), both)

    def multiply(n):
        first = (M,) not in seen
        seen.add((M,))
        part = weigh(CHUNKS[n], sc)
        if first:
            sums[...] = part
        else:
            sums[...] += part

        @pl.loop(0, 2)
        def _(i):
            at = pl.ds(pl.multiple_of(i * half, half), half)
            left = rows_of(rp, CHUNKS[n], at)
            for j in range(half // 256):
                to = pl.ds(j * 256, 256)
                part = over_rows(left, sc[:, to])
                if first:
                    acc[at, to] = part
                else:
                    acc[at, to] += part

    for one in ORDER:
        step(*one)
    got(product_needs(LAST) + [(READY, d) for d in near])
    sums[...] += weigh(LAST, last)
    for c in copies.values():
        c.wait_send()


def finish(acc, sums, rp, last, gram_hbm, means_hbm, out, means, sems):
    rows, half = acc.shape
    total = 16 * 8 * rp.shape[3]
    means[...] = sums[:64, :128] / (sums[:64, 128:] + 1.0)
    writes = [pltpu.make_async_copy(means, means_hbm, sems.at[0])]
    writes[0].start()
    for i in range(rows // 128):
        at = pl.ds(i * 128, 128)
        left = rows_of(rp, LAST, at)
        for j in range(half // 1024):
            to = pl.ds(j * 1024, 1024)
            out[at, to] = (acc[at, to] + over_rows(left, last[:, to])) / float(total)
            n = len(writes)
            writes.append(pltpu.make_async_copy(out.at[at, to], gram_hbm.at[at, to], sems.at[n]))
            writes[n].start()
    for w in writes:
        w.wait()


def body(activations, labels, valid, class_weight):
    tok, width = activations.shape
    classes = class_weight.shape[0]
    block = width // 8
    half = block // 2
    chunk = 2 * 8 * tok
    vmem = pl.BlockSpec(memory_space=pltpu.VMEM)
    hbm = pl.BlockSpec(memory_space=pltpu.HBM)
    parts = pl.pallas_call(
        exchange,
        out_shape=(
            pltpu.VMEM((block, half), jnp.float32),
            pltpu.VMEM((128, 256), jnp.float32),
            pltpu.VMEM((16, 2, 4, tok, block), jnp.bfloat16),
            pltpu.VMEM((chunk, half), jnp.bfloat16),
        ),
        in_specs=[hbm] * 4,
        out_specs=(vmem,) * 4,
        scratch_shapes=[
            pltpu.VMEM((16, 2, 4, tok, half), jnp.bfloat16),
            pltpu.VMEM((4, 2, tok, half), jnp.bfloat16),
            pltpu.VMEM((chunk, half), jnp.bfloat16),
            pltpu.VMEM((4, 4, 2, 4, 1, 128), jnp.float32),
            pltpu.VMEM((1, tok), jnp.int32),
            pltpu.VMEM((1, tok), jnp.int32),
            pltpu.VMEM((1, classes), jnp.float32),
            pltpu.SemaphoreType.DMA((160,)),
            pltpu.SemaphoreType.DMA((160,)),
            pltpu.SemaphoreType.DMA((6,)),
            pltpu.SemaphoreType.REGULAR((7,)),
            pltpu.SemaphoreType.REGULAR((7,)),
        ],
        compiler_params=pltpu.CompilerParams(
            collective_id=0, has_side_effects=True, vmem_limit_bytes=12 * 1024 * 1024
        ),
    )(
        *[
            pltpu.with_memory_space_constraint(a, pltpu.HBM)
            for a in (
                activations,
                labels.reshape(1, tok),
                valid.reshape(1, tok),
                class_weight.reshape(1, classes),
            )
        ]
    )
    return pl.pallas_call(
        finish,
        out_shape=(
            jax.ShapeDtypeStruct((block, half), jnp.float32),
            jax.ShapeDtypeStruct((classes, 128), jnp.float32),
        ),
        in_specs=[vmem] * 4,
        out_specs=(hbm, hbm),
        scratch_shapes=[
            pltpu.VMEM((block, half), jnp.float32),
            pltpu.VMEM((classes, 128), jnp.float32),
            pltpu.SemaphoreType.DMA((17,)),
        ],
        compiler_params=pltpu.CompilerParams(vmem_limit_bytes=14 * 1024 * 1024),
    )(*parts)


def solution(mesh):
    in_specs = (P(("row", "col"), None), P(("row", "col")), P(("row", "col")), P())
    out_specs = (P("row", "col"), P(None, ("row", "col")))
    return jax.shard_map(body, mesh=mesh, in_specs=in_specs, out_specs=out_specs, check_vma=False)
```
